32 devices in a mesh: expert: 4 (over x, core), seq: 2 (over y), tensor: 4 (over z).
Axes of the slice: x: 2, y: 2, z: 4, core: 2. Of those that a mesh axis runs over, the one named last changes fastest.
Arguments:
- tokens_in: bfloat16 [128, 6144], P(('expert', 'seq'), 'tensor'), may hold values from -6 to 6
- out_grad: bfloat16 [128, 6144], P(('expert', 'seq'), 'tensor'), may hold values from -6 to 6
- route_ids: int32 [128, 2], P(('expert', 'seq')), may hold values from 0 to 3, all different within a row; in each aligned block of 16 rows (0 to 15, 16 to 31, ...) at most 16 rows name the same one
- route_weight: bfloat16 [128, 2], P(('expert', 'seq')), may hold values from 0.099609375 to 1
- gate_weight: bfloat16 [4, 6144, 8192], P('expert', None, ('seq', 'tensor')), may hold values from -0.078125 to 0.078125
- up_weight: bfloat16 [4, 6144, 8192], P('expert', None, ('seq', 'tensor')), may hold values from -0.078125 to 0.078125
- down_weight: bfloat16 [4, 8192, 6144], P('expert', ('seq', 'tensor')), may hold values from -0.0625 to 0.0625
Outputs:
- x_grad: bfloat16 [128, 6144], P(('expert', 'seq'), 'tensor')
- route_grad: bfloat16 [128, 2], P(('expert', 'seq'))
- gate_grad: bfloat16 [4, 6144, 8192], P('expert', None, ('seq', 'tensor'))
- up_grad: bfloat16 [4, 6144, 8192], P('expert', None, ('seq', 'tensor'))
- down_grad: bfloat16 [4, 8192, 6144], P('expert', ('seq', 'tensor'))
The draws below stay inside these ranges and needn't reach their ends.
Inputs may be any that keep to these rules, and one draw needn't show every extreme that they name: `route_ids`: each token names two different experts, and every expert is named by some token.
All inputs are finite; a program needn't handle non-finite values.
Results may differ from the reference program's by a relative error of at most 0.0059.
Values may be sent and summed in bfloat16 or wider, within the bound.
No kernel may reach another device: no remote copies, remote signals or barrier semaphores. Data moves between devices by JAX's collectives and lax.ppermute only.
A program may use at most 192 MiB of HBM per device.

```python
import math
import jax
import jax.numpy as jnp
import numpy as np
from jax import lax

D = 6144
FF = 8192
EXPERTS = 4
TOK_SHARD = 16
TOKENS = 128


def block_levels(key, extent, cuts, low, high):
    loudness = 1.0
    for position, shards_of in cuts:
        heights = jax.random.uniform(jax.random.fold_in(jax.random.fold_in(key, 6), position), (shards_of,), jnp.float32, low / len(cuts), high / len(cuts))
        loudness = loudness * jnp.repeat(jnp.exp(heights), extent[position] // shards_of).reshape((-1,) + (1,) * (len(extent) - 1 - position))
    return loudness


def shared_out(rng, own, number, rows, amount, top, reach, skew):
    sequence = jax.random.permutation(rng, amount)
    packed, usual = shares(amount, rows * top, reach, skew, True), shares(amount, rows * top, reach, skew, False)
    places = jnp.arange(amount)

    def named(lengths, rotation):
        used = int((lengths > 0).sum())
        fixed = max(1, used // 4)
        shifted = fixed + (places - fixed + rotation * (used - fixed)) % max(1, amount - fixed)
        return jnp.zeros((amount,), jnp.int32).at[sequence[jnp.where(places < fixed, places, shifted)]].set(jnp.asarray(lengths, jnp.int32))

    lengths = jnp.where(number % 4 == 0, named(packed, number // 4), named(usual, number - number // 4 - 1))
    mixed = jax.random.permutation(jax.random.fold_in(own, 3), amount)
    source_of, receiver = mixed[0:amount // 2 * 2:2], mixed[1:amount // 2 * 2:2]
    slack = jnp.minimum(lengths[source_of] - 1, reach - lengths[receiver]) // 2
    slack = jnp.where((source_of == sequence[0]) | (receiver == sequence[0]) | (lengths[receiver] == 0), 0, jnp.maximum(slack, 0))
    shifted = jax.random.randint(jax.random.fold_in(own, 4), (amount // 2,), 0, 1 << 20) % (slack + 1)
    lengths = lengths.at[source_of].add(-shifted).at[receiver].add(shifted)
    items = jnp.searchsorted(jnp.cumsum(lengths), jnp.arange(rows * top), side="right").astype(jnp.int32)
    table = items.reshape(top, rows).T
    table = table[jax.random.permutation(jax.random.fold_in(own, 1), rows)]
    rotation = jax.random.randint(jax.random.fold_in(own, 2), (rows, 1), 0, top)
    return jnp.take_along_axis(table, (jnp.arange(top)[None, :] + rotation) % top, axis=1)


def shares(number_of, total, most, slope, full):
    loads = [(1 << 20) // math.isqrt(rank ** slope) + 1 for rank in range(1, number_of + 1)]
    largest = most if full else min(most, max(-(-total // number_of), total * loads[0] // sum(loads)))
    least = 1 if total - largest >= number_of - 1 else 0
    counts, rest = [largest] + [least] * (number_of - 1), total - largest - least * (number_of - 1)
    while rest > 0:
        free = [i for i in range(1, number_of) if counts[i] < largest] or [i for i in range(1, number_of) if counts[i] < most]
        mass, remaining = sum([loads[i] for i in free]), rest
        for i in free:
            extra = min(most - counts[i], max(1, remaining * loads[i] // mass), rest)
            counts[i] = counts[i] + extra
            rest = rest - extra
    return np.array(counts)


def scatter_about(rng, shape, deviation, most, cuts=(), dtype=jnp.bfloat16):
    loudness = block_levels(rng, shape, cuts, -0.22, 0.18) if cuts else 1.0
    result = jax.random.normal(rng, shape, jnp.float32) * deviation * loudness
    return jnp.minimum(jnp.maximum(result, -most), most).astype(dtype)


def setup_inputs(seed: int = 0) -> dict:
    seeds = jax.random.split(jax.random.key(seed), 8)
    tokens_in = scatter_about(seeds[0], (TOKENS, D), 1.0, 6.0, ((0, 8), (1, 4)))
    out_grad = scatter_about(seeds[1], (TOKENS, D), 1.0, 6.0, ((0, 8), (1, 4)))
    route_ids_keys = jax.random.split(jax.random.fold_in(seeds[2], 1), TOKENS // TOK_SHARD)
    route_ids_turns = jax.random.permutation(jax.random.fold_in(seeds[2], 3), TOKENS // TOK_SHARD)
    route_ids = jax.vmap(lambda own, number: shared_out(jax.random.fold_in(seeds[2], 2), own, number, TOK_SHARD, EXPERTS, 2, TOK_SHARD, 2))(route_ids_keys, route_ids_turns).reshape((TOKENS, 2))
    route_weight = jnp.clip(jnp.exp(math.log(1.0) - 2.306499 * jax.random.uniform(seeds[3], (TOKENS, 2), jnp.float32) ** block_levels(seeds[3], (TOKENS, 2), ((0, 8),), -0.2, 0.2)), 0.099609375, 1.0).astype(jnp.bfloat16)
    gate_weight = scatter_about(seeds[4], (EXPERTS, D, FF), D ** -0.5, 0.078125, ((0, 4), (2, 8)))
    up_weight = scatter_about(seeds[5], (EXPERTS, D, FF), D ** -0.5, 0.078125, ((0, 4), (2, 8)))
    down_weight = scatter_about(seeds[6], (EXPERTS, FF, D), FF ** -0.5, 0.0625, ((0, 4), (1, 8)))
    return dict(tokens_in=tokens_in, out_grad=out_grad, route_ids=route_ids, route_weight=route_weight, gate_weight=gate_weight, up_weight=up_weight, down_weight=down_weight)


def reference(tokens_in, out_grad, route_ids, route_weight, gate_weight, up_weight, down_weight):
    contract_rows = (((0,), (0,)), ((), ()))
    contract_cols = (((1,), (1,)), ((), ()))
    x_total = jnp.zeros(tokens_in.shape, jnp.float32)
    route_total = jnp.zeros(route_ids.shape, jnp.float32)
    gate_grads = []
    up_grads = []
    down_grads = []
    for expert in range(EXPERTS):
        chosen = (route_ids == expert).astype(jnp.float32)
        row_weight = jnp.sum(chosen * route_weight.astype(jnp.float32), axis=1, keepdims=True)
        gate_value = jnp.dot(tokens_in, gate_weight[expert], preferred_element_type=jnp.float32)
        up_value = jnp.dot(tokens_in, up_weight[expert], preferred_element_type=jnp.float32)
        sigmoid_gate = jax.nn.sigmoid(gate_value)
        activated = gate_value * sigmoid_gate
        hidden_value = activated * up_value
        raw_grad = lax.dot_general(out_grad, down_weight[expert], contract_cols, preferred_element_type=jnp.float32)
        route_part = jnp.sum(hidden_value * raw_grad, axis=1).astype(jnp.bfloat16)
        route_part = lax.optimization_barrier(route_part)
        scaled = row_weight * raw_grad
        gate_delta = (scaled * up_value * sigmoid_gate * (1.0 + gate_value * (1.0 - sigmoid_gate))).astype(jnp.bfloat16)
        up_delta = (scaled * activated).astype(jnp.bfloat16)
        hidden_scaled = (row_weight * hidden_value).astype(jnp.bfloat16)
        gate_grads.append(lax.dot_general(tokens_in, gate_delta, contract_rows, preferred_element_type=jnp.float32).astype(jnp.bfloat16))
        up_grads.append(lax.dot_general(tokens_in, up_delta, contract_rows, preferred_element_type=jnp.float32).astype(jnp.bfloat16))
        down_grads.append(lax.dot_general(hidden_scaled, out_grad, contract_rows, preferred_element_type=jnp.float32).astype(jnp.bfloat16))
        input_delta = lax.dot_general(gate_delta, gate_weight[expert], contract_cols, preferred_element_type=jnp.float32)
        input_delta = input_delta + lax.dot_general(up_delta, up_weight[expert], contract_cols, preferred_element_type=jnp.float32)
        input_delta = lax.optimization_barrier(input_delta.astype(jnp.bfloat16))
        used = jnp.sum(chosen, axis=1, keepdims=True)
        x_total = x_total + used * input_delta.astype(jnp.float32)
        route_total = route_total + chosen * route_part.astype(jnp.float32)[:, None]
    return (x_total.astype(jnp.bfloat16), route_total.astype(jnp.bfloat16),
            jnp.stack(gate_grads), jnp.stack(up_grads), jnp.stack(down_grads))
```

```python
import functools

import jax
import jax.numpy as jnp
from jax import lax
from jax.experimental import pallas as pl
from jax.experimental.pallas import tpu as pltpu
from jax.sharding import PartitionSpec as P

EXTRA = 128
MIB = 1 << 20
CONTRACT_ROWS = (((0,), (0,)), ((), ()))
CONTRACT_COLS = (((1,), (1,)), ((), ()))


def params(mib):
    return pltpu.CompilerParams(vmem_limit_bytes=mib * MIB)


def cost(flops, moved):
    return pl.CostEstimate(flops=int(flops), bytes_accessed=int(moved), transcendentals=0)


def chunk_of(features):
    for size in (768, 512, 384, 256, 128):
        if features % size == 0:
            return size
    return features


def relative_chunk(step, home, pieces, per_piece):
    owner = step // per_piece
    return lax.rem(home - owner + pieces, pieces) * per_piece + lax.rem(step, per_piece)


def matmul(a, b, dims=None):
    if dims is None:
        return jnp.dot(a, b, preferred_element_type=jnp.float32)
    return lax.dot_general(a, b, dims, preferred_element_type=jnp.float32)


def gate_up_kernel(home, xp, xo, wg, wu, gate, up):
    @pl.when(pl.program_id(0) == 0)
    def _():
        gate[...] = jnp.zeros_like(gate)
        up[...] = jnp.zeros_like(up)

    rows = jnp.concatenate([xp[...], xo[...]], axis=0)
    gate[...] += matmul(rows, wg[0])
    up[...] += matmul(rows, wu[0])


def gate_up(home, pieces, near, far, w_gate, w_up):
    half = near.shape[0]
    _, depth, hidden = w_gate.shape
    size = chunk_of(depth // pieces)
    per_piece = depth // pieces // size
    rel = functools.partial(relative_chunk, pieces=pieces, per_piece=per_piece)
    out = jax.ShapeDtypeStruct((2 * half, hidden), jnp.float32)
    rows = pl.BlockSpec((half, size), lambda j, home: (0, rel(j, home[0])))
    weights = pl.BlockSpec((1, size, hidden), lambda j, home: (0, j, 0))
    whole = pl.BlockSpec((2 * half, hidden), lambda j, home: (0, 0))
    return pl.pallas_call(
        gate_up_kernel,
        grid_spec=pltpu.PrefetchScalarGridSpec(
            num_scalar_prefetch=1,
            grid=(depth // size,),
            in_specs=[rows, rows, weights, weights],
            out_specs=[whole, whole],
        ),
        out_shape=[out, out],
        compiler_params=params(32),
        cost_estimate=cost(8 * half * depth * hidden, 4 * depth * hidden),
        name="gate_up",
    )(home, near, far, w_gate, w_up)


def delta_kernel(home, me, gp, go, wd, gate, up, xpw, xow, dgate, dup, hidw, part, raw, *, experts):
    step = pl.program_id(0)

    @pl.when(step == 0)
    def _():
        raw[...] = jnp.zeros_like(raw)

    rows = jnp.concatenate([gp[...], go[...]], axis=0)
    raw[...] += matmul(rows, wd[0], CONTRACT_COLS)

    @pl.when(step == pl.num_programs(0) - 1)
    def _():
        lane = lax.broadcasted_iota(jnp.int32, (1, EXTRA), 1)
        weights = jnp.concatenate([xpw[...], xow[...]], axis=0).astype(jnp.float32)
        mine = lane == me[0]
        weight = jnp.sum(jnp.where(mine, weights, 0.0), axis=1, keepdims=True)
        gate_value = gate[...]
        up_value = up[...]
        raw_value = raw[...]
        sigmoid_gate = jax.nn.sigmoid(gate_value)
        activated = gate_value * sigmoid_gate
        hidden_value = activated * up_value
        scaled = weight * raw_value
        slope = sigmoid_gate * (1.0 + gate_value * (1.0 - sigmoid_gate))
        dgate[...] = (scaled * up_value * slope).astype(jnp.bfloat16)
        dup[...] = (scaled * activated).astype(jnp.bfloat16)
        hidw[...] = (weight * hidden_value).astype(jnp.bfloat16)
        total = jnp.sum(hidden_value * raw_value, axis=1, keepdims=True)
        high = total.astype(jnp.bfloat16).astype(jnp.float32)
        low = total - high
        placed = jnp.where(mine, high, 0.0) + jnp.where(lane == me[0] + experts, low, 0.0)
        part[...] = placed.astype(jnp.bfloat16)


def deltas(home, me, experts, pieces, near, far, w_down, gate, up, near_x, far_x):
    half = near.shape[0]
    _, hidden, depth = w_down.shape
    size = chunk_of(depth // pieces)
    per_piece = depth // pieces // size
    rel = functools.partial(relative_chunk, pieces=pieces, per_piece=per_piece)
    rows = pl.BlockSpec((half, size), lambda j, home, me: (0, rel(j, home[0])))
    weights = pl.BlockSpec((1, hidden, size), lambda j, home, me: (0, 0, j))
    whole = pl.BlockSpec((2 * half, hidden), lambda j, home, me: (0, 0))
    extra_in = pl.BlockSpec((half, EXTRA), lambda j, home, me: (0, depth // EXTRA))
    extra_out = pl.BlockSpec((2 * half, EXTRA), lambda j, home, me: (0, 0))
    out = jax.ShapeDtypeStruct((2 * half, hidden), jnp.bfloat16)
    return pl.pallas_call(
        functools.partial(delta_kernel, experts=experts),
        grid_spec=pltpu.PrefetchScalarGridSpec(
            num_scalar_prefetch=2,
            grid=(depth // size,),
            in_specs=[rows, rows, weights, whole, whole, extra_in, extra_in],
            out_specs=[whole, whole, whole, extra_out],
            scratch_shapes=[pltpu.VMEM((2 * half, hidden), jnp.float32)],
        ),
        out_shape=[out, out, out, jax.ShapeDtypeStruct((2 * half, EXTRA), jnp.bfloat16)],
        compiler_params=params(32),
        cost_estimate=cost(4 * half * depth * hidden, 2 * depth * hidden),
        name="deltas",
    )(home, me, near, far, w_down, gate, up, near_x, far_x)


def input_kernel(home, dgate, dup, wg, wu, part, near, far, *, pieces, per_piece):
    step = pl.program_id(0)
    size = wg.shape[1]
    half = near.shape[0]
    depth = near.shape[1] - EXTRA
    value = matmul(dgate[...], wg[0], CONTRACT_COLS) + matmul(dup[...], wu[0], CONTRACT_COLS)
    value = value.astype(jnp.bfloat16)
    start = pl.multiple_of(relative_chunk(step, home[0], pieces, per_piece) * size, size)
    near[:, pl.ds(start, size)] = value[:half]
    far[:, pl.ds(start, size)] = value[half:]

    @pl.when(step == 0)
    def _():
        near[:, depth:] = part[:half, :]
        far[:, depth:] = part[half:, :]


def input_grads(home, pieces, dgate, dup, w_gate, w_up, part):
    rows, hidden = dgate.shape
    half = rows // 2
    depth = w_gate.shape[1]
    size = chunk_of(depth // pieces)
    per_piece = depth // pieces // size
    weights = pl.BlockSpec((1, size, hidden), lambda j, home: (0, j, 0))
    whole = pl.BlockSpec((rows, hidden), lambda j, home: (0, 0))
    extra = pl.BlockSpec((rows, EXTRA), lambda j, home: (0, 0))
    result = pl.BlockSpec((half, depth + EXTRA), lambda j, home: (0, 0))
    out = jax.ShapeDtypeStruct((half, depth + EXTRA), jnp.bfloat16)
    return pl.pallas_call(
        functools.partial(input_kernel, pieces=pieces, per_piece=per_piece),
        grid_spec=pltpu.PrefetchScalarGridSpec(
            num_scalar_prefetch=1,
            grid=(depth // size,),
            in_specs=[whole, whole, weights, weights, extra],
            out_specs=[result, result],
        ),
        out_shape=[out, out],
        compiler_params=params(32),
        cost_estimate=cost(4 * rows * depth * hidden, 4 * depth * hidden),
        name="input_grads",
    )(home, dgate, dup, w_gate, w_up, part)


def columns_kernel(home, xp, xo, delta, out):
    rows = jnp.concatenate([xp[...], xo[...]], axis=0)
    out[0] = matmul(rows, delta[...], CONTRACT_ROWS).astype(jnp.bfloat16)


def columns_grad(home, pieces, near, far, delta, depth):
    half = near.shape[0]
    hidden = delta.shape[1]
    size = chunk_of(depth // pieces)
    per_piece = depth // pieces // size
    rel = functools.partial(relative_chunk, pieces=pieces, per_piece=per_piece)
    rows = pl.BlockSpec((half, size), lambda j, home: (0, rel(j, home[0])))
    return pl.pallas_call(
        columns_kernel,
        grid_spec=pltpu.PrefetchScalarGridSpec(
            num_scalar_prefetch=1,
            grid=(depth // size,),
            in_specs=[rows, rows, pl.BlockSpec((2 * half, hidden), lambda j, home: (0, 0))],
            out_specs=pl.BlockSpec((1, size, hidden), lambda j, home: (0, j, 0)),
        ),
        out_shape=jax.ShapeDtypeStruct((1, depth, hidden), jnp.bfloat16),
        compiler_params=params(32),
        cost_estimate=cost(4 * half * depth * hidden, 2 * depth * hidden),
        name="columns_grad",
    )(home, near, far, delta)


def down_kernel(home, gp, go, hidw, out):
    rows = jnp.concatenate([gp[...], go[...]], axis=0)
    out[0] = matmul(hidw[...], rows, CONTRACT_ROWS).astype(jnp.bfloat16)


def down_grads(home, pieces, near, far, hidw, depth):
    half = near.shape[0]
    hidden = hidw.shape[1]
    size = chunk_of(depth // pieces)
    per_piece = depth // pieces // size
    rel = functools.partial(relative_chunk, pieces=pieces, per_piece=per_piece)
    rows = pl.BlockSpec((half, size), lambda j, home: (0, rel(j, home[0])))
    return pl.pallas_call(
        down_kernel,
        grid_spec=pltpu.PrefetchScalarGridSpec(
            num_scalar_prefetch=1,
            grid=(depth // size,),
            in_specs=[rows, rows, pl.BlockSpec((2 * half, hidden), lambda j, home: (0, 0))],
            out_specs=pl.BlockSpec((1, hidden, size), lambda j, home: (0, 0, j)),
        ),
        out_shape=jax.ShapeDtypeStruct((1, hidden, depth), jnp.bfloat16),
        compiler_params=params(32),
        cost_estimate=cost(4 * half * depth * hidden, 2 * depth * hidden),
        name="down_grads",
    )(home, near, far, hidw)


def resplit(extra, experts):
    total = extra[:, :experts] + extra[:, experts : 2 * experts]
    high = total.astype(jnp.bfloat16)
    low = (total - high.astype(jnp.float32)).astype(jnp.bfloat16)
    rest = jnp.zeros((extra.shape[0], EXTRA - 2 * experts), jnp.bfloat16)
    return jnp.concatenate([high, low, rest], axis=1)


def tree_sum(parts):
    while len(parts) > 1:
        middle = len(parts) // 2
        parts = [a + b for a, b in zip(parts[:middle], parts[middle:], strict=True)]
    return parts[0]


def per_device(tokens_in, out_grad, route_ids, route_weight, gate_weight, up_weight, down_weight):
    experts = lax.axis_size("expert")
    seqs = lax.axis_size("seq")
    pieces = lax.axis_size("tensor")
    rows, width = tokens_in.shape
    depth = width * pieces
    home = lax.axis_index("tensor").astype(jnp.int32).reshape(1)
    me = lax.axis_index("expert").astype(jnp.int32).reshape(1)
    chips = experts // 2
    planes = [(dx, ds) for ds in range(seqs) for dx in range(chips)]

    def along(value, shift):
        pairs = [(i, (i + shift) % pieces) for i in range(pieces)]
        return lax.ppermute(value, "tensor", pairs)

    def across(value, dx, ds):
        pairs = []
        for e in range(experts):
            for s in range(seqs):
                to_e = ((e // 2 + dx) % chips) * 2 + e % 2
                pairs.append((e * seqs + s, to_e * seqs + (s + ds) % seqs))
        return lax.ppermute(value, ("expert", "seq"), pairs)

    def swap(value):
        return lax.ppermute(value, "expert", [(e, e ^ 1) for e in range(experts)])

    def gather(value, extra):
        blocks = [value] + [along(value, k) for k in range(1, pieces)] + extra
        line = jnp.concatenate(blocks, axis=1)
        near = jnp.concatenate([line] + [across(line, dx, ds) for dx, ds in planes[1:]], axis=0)
        return near, swap(near)

    expert_ids = jnp.arange(EXTRA, dtype=jnp.int32)
    chosen = (route_ids[:, :, None] == expert_ids[None, None, :]).astype(jnp.float32)
    weights = jnp.sum(chosen * route_weight.astype(jnp.float32)[:, :, None], axis=1)
    near_x, far_x = gather(tokens_in, [weights.astype(jnp.bfloat16)])
    near_g, far_g = gather(out_grad, [])

    gate, up = gate_up(home, pieces, near_x, far_x, gate_weight, up_weight)
    dgate, dup, hidw, part = deltas(
        home, me, experts, pieces, near_g, far_g, down_weight, gate, up, near_x, far_x
    )
    near_d, far_d = input_grads(home, pieces, dgate, dup, gate_weight, up_weight, part)

    other_d = swap(far_d)
    wide = near_d.astype(jnp.float32) + other_d.astype(jnp.float32)
    both = jnp.concatenate(
        [wide[:, :depth].astype(jnp.bfloat16), resplit(wide[:, depth:], experts)], axis=1
    )
    blocks = [both[i * rows : (i + 1) * rows] for i in range(len(planes))]
    arrived = [
        across(block, -dx, -ds) for block, (dx, ds) in zip(blocks[1:], planes[1:], strict=True)
    ]
    wide = sum([b.astype(jnp.float32) for b in arrived], blocks[0].astype(jnp.float32))
    line = wide[:, :depth].astype(jnp.bfloat16)
    extra = resplit(wide[:, depth:], experts)
    sends = [
        jnp.concatenate([line[:, k * width : (k + 1) * width], extra], axis=1)
        for k in range(pieces)
    ]
    finals = [sends[0]] + [along(sends[k], -k) for k in range(1, pieces)]
    total = tree_sum([f.astype(jnp.float32) for f in finals])
    x_grad = total[:, :width].astype(jnp.bfloat16)
    routes = total[:, width : width + experts] + total[:, width + experts : width + 2 * experts]
    routes = routes.astype(jnp.bfloat16).astype(jnp.float32)
    route_grad = jnp.sum(chosen[:, :, :experts] * routes[:, None, :], axis=2).astype(jnp.bfloat16)

    gate_grad = columns_grad(home, pieces, near_x, far_x, dgate, depth)
    up_grad = columns_grad(home, pieces, near_x, far_x, dup, depth)
    down_grad = down_grads(home, pieces, near_g, far_g, hidw, depth)
    return (x_grad, route_grad, gate_grad, up_grad, down_grad)


def solution(mesh):
    in_specs = (
        P(("expert", "seq"), "tensor"),
        P(("expert", "seq"), "tensor"),
        P(("expert", "seq"), None),
        P(("expert", "seq"), None),
        P("expert", None, ("seq", "tensor")),
        P("expert", None, ("seq", "tensor")),
        P("expert", ("seq", "tensor"), None),
    )
    out_specs = (
        P(("expert", "seq"), "tensor"),
        P(("expert", "seq"), None),
        P("expert", None, ("seq", "tensor")),
        P("expert", None, ("seq", "tensor")),
        P("expert", ("seq", "tensor"), None),
    )
    return jax.shard_map(
        per_device, mesh=mesh, in_specs=in_specs, out_specs=out_specs, check_vma=False
    )
```

```python
import functools

import jax
import jax.numpy as jnp
from jax import lax
from jax.experimental import pallas as pl
from jax.experimental.pallas import tpu as pltpu
from jax.sharding import PartitionSpec as P

EXTRA = 128
MIB = 1 << 20
PLAIN = (((1,), (0,)), ((), ()))
CONTRACT_ROWS = (((0,), (0,)), ((), ()))
CONTRACT_COLS = (((1,), (1,)), ((), ()))
VMEM = pl.BlockSpec(memory_space=pltpu.VMEM)
SMEM = pl.BlockSpec(memory_space=pltpu.SMEM)
ANY = pl.BlockSpec(memory_space=pl.ANY)
HBM = pl.BlockSpec(memory_space=pltpu.HBM)


def matmul(a, b, dims=PLAIN):
    return lax.dot_general(a, b, dims, preferred_element_type=jnp.float32)


def shaped(shape, dtype=jnp.bfloat16):
    return jax.ShapeDtypeStruct(shape, dtype)


def local_call(
    body, name, mib, flops, moved, in_specs, out_specs, out_shape, scratch=(), aliases=None
):
    return pl.pallas_call(
        body,
        in_specs=in_specs,
        out_specs=out_specs,
        out_shape=out_shape,
        scratch_shapes=list(scratch),
        input_output_aliases=aliases or {},
        compiler_params=pltpu.CompilerParams(vmem_limit_bytes=mib * MIB),
        cost_estimate=pl.CostEstimate(
            flops=int(flops), bytes_accessed=int(moved), transcendentals=0
        ),
        name=name,
    )


def chunk_of(features):
    for size in (768, 512, 384, 256, 128):
        if features % size == 0:
            return size
    return features


def whole_chunks(home, pieces, depth):
    width = depth // pieces
    size = chunk_of(width)
    found = []
    for k in range(pieces):
        owner = lax.rem(home - k + pieces, pieces)
        for c in range(width // size):
            start = pl.multiple_of(owner * width + c * size, size)
            found.append((k * width + c * size, start))
    return size, found


def both_rows(near, far, start, size):
    return jnp.concatenate([near[:, start : start + size], far[:, start : start + size]], axis=0)


def turned_kernel(place, w, *refs, pieces, by_rows, first, count):
    *outs, buf, sems = refs[-count - 2 :]
    depth = w.shape[1] if by_rows else w.shape[2]
    width = depth // pieces
    size, chunks = whole_chunks(place[0], pieces, depth)
    chunks = [c for c in chunks if first <= c[0] // width < first + count]
    slots = buf.shape[0]

    def copy(j):
        span = pl.ds(chunks[j][1], size)
        source = w.at[0, span] if by_rows else w.at[0, :, span]
        return pltpu.make_async_copy(source, buf.at[j % slots], sems.at[j % slots])

    for j in range(min(slots, len(chunks))):
        copy(j).start()
    for j, (rel, _) in enumerate(chunks):
        copy(j).wait()
        out, base = outs[rel // width - first], rel % width
        for at in range(0, buf.shape[2], EXTRA):
            value = buf[j % slots, :, at : at + EXTRA].T
            if by_rows:
                out[at : at + EXTRA, base : base + size] = value
            else:
                out[base + at : base + at + EXTRA, :] = value
        if j + slots < len(chunks):
            copy(j + slots).start()


def turned(place, pieces, weights, by_rows, which, after=()):
    _, up_to, across = weights.shape
    depth, hidden = (up_to, across) if by_rows else (across, up_to)
    width = depth // pieces
    size = chunk_of(width)
    shape = (hidden, width) if by_rows else (width, hidden)
    return local_call(
        functools.partial(
            turned_kernel, pieces=pieces, by_rows=by_rows, first=which.start, count=len(which)
        ),
        "turned",
        8,
        0,
        0,
        [SMEM, HBM] + [ANY] * len(after),
        [VMEM] * len(which),
        [shaped(shape)] * len(which),
        [
            pltpu.VMEM((4, size, hidden) if by_rows else (4, hidden, size), jnp.bfloat16),
            pltpu.SemaphoreType.DMA((4,)),
        ],
    )(place, pltpu.with_memory_space_constraint(weights, pltpu.HBM), *after)


def gate_up_kernel(place, xp, xo, *refs, pieces):
    weights, (gate, up, weight) = refs[: 2 * pieces], refs[2 * pieces :]
    hidden, width = weights[0].shape
    for half, out in ((weights[:pieces], gate), (weights[pieces:], up)):
        for k, w in enumerate(half):
            rows = both_rows(xp, xo, k * width, width)
            for at in range(0, hidden, EXTRA):
                value = matmul(rows, w[at : at + EXTRA, :], CONTRACT_COLS)
                if k == 0:
                    out[:, at : at + EXTRA] = value
                else:
                    out[:, at : at + EXTRA] += value
    lane = lax.broadcasted_iota(jnp.int32, (1, EXTRA), 1)
    mine = both_rows(xp, xo, width * pieces, EXTRA).astype(jnp.float32)
    total = jnp.sum(jnp.where(lane == place[1], mine, 0.0), axis=1, keepdims=True)
    weight[...] = jnp.broadcast_to(total, weight.shape)


def gate_up(place, near, far, turned_gate, turned_up):
    half = near.shape[0]
    pieces = len(turned_gate)
    hidden = turned_gate[0].shape[0]
    out = shaped((2 * half, hidden), jnp.float32)
    return local_call(
        functools.partial(gate_up_kernel, pieces=pieces),
        "gate_up",
        3,
        0,
        0,
        [SMEM] + [VMEM] * (2 + 2 * pieces),
        [VMEM] * 3,
        [out, out, shaped((2 * half, EXTRA), jnp.float32)],
    )(place, near, far, *turned_gate, *turned_up)


def middle_kernel(
    place, gp, go, weight_in, gate, up, *refs, pieces, experts
):
    wd, wg, wu = refs[:pieces], refs[pieces : 2 * pieces], refs[2 * pieces : 3 * pieces]
    near, far, dgate, dup, hidw, raw = refs[3 * pieces :]
    width = wg[0].shape[1]
    half = near.shape[0]
    depth = width * pieces
    for k in range(pieces):
        value = matmul(both_rows(gp, go, k * width, width), wd[k][...])
        if k == 0:
            raw[...] = value
        else:
            raw[...] += value
    lane = lax.broadcasted_iota(jnp.int32, (1, EXTRA), 1)
    mine = lane == place[1]
    weight = weight_in[:, :1]
    gate_value = gate[...]
    up_value = up[...]
    raw_value = raw[...]
    sigmoid_gate = jax.nn.sigmoid(gate_value)
    activated = gate_value * sigmoid_gate
    hidden_value = activated * up_value
    scaled = weight * raw_value
    slope = sigmoid_gate * (1.0 + gate_value * (1.0 - sigmoid_gate))
    dgate[...] = (scaled * up_value * slope).astype(jnp.bfloat16)
    dup[...] = (scaled * activated).astype(jnp.bfloat16)
    hidw[...] = (weight * hidden_value).astype(jnp.bfloat16)
    total = jnp.sum(hidden_value * raw_value, axis=1, keepdims=True)
    high = total.astype(jnp.bfloat16).astype(jnp.float32)
    low = total - high
    placed = jnp.where(mine, high, 0.0) + jnp.where(lane == place[1] + experts, low, 0.0)
    placed = placed.astype(jnp.bfloat16)
    near[:, depth:] = placed[:half]
    far[:, depth:] = placed[half:]
    step = chunk_of(width)
    for at in range(0, depth, step):
        k, base = at // width, at % width
        span = slice(base, base + step)
        value = matmul(dgate[...], wg[k][:, span]) + matmul(dup[...], wu[k][:, span])
        value = value.astype(jnp.bfloat16)
        near[:, at : at + step] = value[:half]
        far[:, at : at + step] = value[half:]


def middle(place, experts, pieces, near, far, weight, gate, up, turned_down, turned_gate, turned_up):
    half = near.shape[0]
    hidden, width = turned_gate[0].shape
    depth = width * pieces
    out = shaped((2 * half, hidden))
    result = shaped((half, depth + EXTRA))
    return local_call(
        functools.partial(middle_kernel, pieces=pieces, experts=experts),
        "middle",
        4,
        0,
        0,
        [SMEM] + [VMEM] * (5 + 3 * pieces),
        [VMEM] * 5,
        [result, result, out, out, out],
        [pltpu.VMEM((2 * half, hidden), jnp.float32)],
    )(place, near, far, weight, gate, up, *turned_down, *turned_gate, *turned_up)


def columns_kernel(place, xp, xo, delta, out, buf, sems, *, pieces):
    depth = out.shape[1]
    size, chunks = whole_chunks(place[0], pieces, depth)
    copies = []
    for j, (rel, start) in enumerate(chunks):
        rows = both_rows(xp, xo, rel, size)
        slot = j
        buf[slot] = matmul(rows, delta[...], CONTRACT_ROWS).astype(jnp.bfloat16)
        copy = pltpu.make_async_copy(
            buf.at[slot], out.at[0, pl.ds(start, size)], sems.at[slot]
        )
        copy.start()
        copies.append(copy)
    for copy in copies:
        copy.wait()


def columns_grad(place, pieces, near, far, delta, depth):
    half = near.shape[0]
    hidden = delta.shape[1]
    count = depth // chunk_of(depth // pieces)
    return local_call(
        functools.partial(columns_kernel, pieces=pieces),
        "columns_grad",
        16,
        4 * half * depth * hidden,
        2 * depth * hidden,
        [SMEM, VMEM, VMEM, VMEM],
        ANY,
        shaped((1, depth, hidden)),
        [
            pltpu.VMEM((count, chunk_of(depth // pieces), hidden), jnp.bfloat16),
            pltpu.SemaphoreType.DMA((count,)),
        ],
    )(place, near, far, delta)


def down_kernel(place, gp, go, hidw, *refs, pieces, first, last):
    out, buf, sems = refs[-3:]
    depth = out.shape[2]
    size, chunks = whole_chunks(place[0], pieces, depth)
    copies = []
    for j, (rel, start) in enumerate(chunks[first:last]):
        rows = both_rows(gp, go, rel, size)
        buf[j] = matmul(hidw[...], rows, CONTRACT_ROWS).astype(jnp.bfloat16)
        copy = pltpu.make_async_copy(buf.at[j], out.at[0, :, pl.ds(start, size)], sems.at[j])
        copy.start()
        copies.append(copy)
    for copy in copies:
        copy.wait()


def down_grads(place, pieces, near, far, hidw, depth, first, last, partial=()):
    half = near.shape[0]
    hidden = hidw.shape[1]
    count = last - first
    size = chunk_of(depth // pieces)
    partial = [pltpu.with_memory_space_constraint(p, pltpu.HBM) for p in partial]
    return local_call(
        functools.partial(down_kernel, pieces=pieces, first=first, last=last),
        "down_grads",
        16,
        4 * half * size * count * hidden,
        2 * size * count * hidden,
        [SMEM, VMEM, VMEM, VMEM] + [HBM] * len(partial),
        ANY,
        shaped((1, hidden, depth)),
        [
            pltpu.VMEM((count, hidden, size), jnp.bfloat16),
            pltpu.SemaphoreType.DMA((count,)),
        ],
        aliases={4: 0} if partial else None,
    )(place, near, far, hidw, *partial)


def stack_kernel(*refs, axis, count):
    out = refs[-1]
    at = 0
    for ref in refs[:count]:
        size = ref.shape[axis]
        if axis:
            out[:, at : at + size] = ref[...]
        else:
            out[at : at + size, :] = ref[...]
        at += size


def stacked(blocks, axis, after=()):
    shape = list(blocks[0].shape)
    shape[axis] = sum(b.shape[axis] for b in blocks)
    count = shape[0] * shape[1]
    return local_call(
        functools.partial(stack_kernel, axis=axis, count=len(blocks)),
        "stacked",
        2,
        0,
        4 * count,
        [VMEM] * len(blocks) + [ANY] * len(after),
        VMEM,
        shaped(tuple(shape)),
    )(*blocks, *after)


def first_kernel(x, g, out, sems):
    rows = x.shape[0]
    copies = [
        pltpu.make_async_copy(ref, out.at[pl.ds(i * rows, rows)], sems.at[i])
        for i, ref in enumerate((x, g))
    ]
    for copy in copies:
        copy.start()
    for copy in copies:
        copy.wait()


def first_pair(x, g):
    rows, width = x.shape
    return local_call(
        first_kernel,
        "first_pair",
        1,
        0,
        8 * rows * width,
        [HBM] * 2,
        VMEM,
        shaped((2 * rows, width)),
        [pltpu.SemaphoreType.DMA((2,))],
    )(*(pltpu.with_memory_space_constraint(v, pltpu.HBM) for v in (x, g)))


def line_pair_kernel(*refs):
    *blocks, extra, _, line_x, line_g = refs
    rows = line_x.shape[0]
    width = blocks[0].shape[1]
    for k, block in enumerate(blocks):
        line_x[:, k * width : (k + 1) * width] = block[:rows, :]
        line_g[:, k * width : (k + 1) * width] = block[rows:, :]
    line_x[:, len(blocks) * width :] = extra[...]


def line_pair(blocks, extra, after):
    rows = extra.shape[0]
    depth = blocks[0].shape[1] * len(blocks)
    return local_call(
        line_pair_kernel,
        "line_pair",
        2,
        0,
        8 * rows * depth,
        [VMEM] * (len(blocks) + 1) + [ANY],
        [VMEM] * 2,
        [shaped((rows, depth + EXTRA)), shaped((rows, depth))],
    )(*blocks, extra, after)


def resplit(extra, experts):
    lane = lax.broadcasted_iota(jnp.int32, extra.shape, 1)
    total = extra + pltpu.roll(extra, EXTRA - experts, 1)
    total = jnp.where(lane < experts, total, 0.0)
    high = total.astype(jnp.bfloat16).astype(jnp.float32)
    return (high + pltpu.roll(total - high, experts, 1)).astype(jnp.bfloat16)


def pair_kernel(near, other, *outs, experts):
    rows, width = outs[0].shape
    depth = width - EXTRA
    for i, out in enumerate(outs):
        span = pl.ds(i * rows, rows)
        value = near[span, :].astype(jnp.float32) + other[span, :].astype(jnp.float32)
        out[:, :depth] = value[:, :depth].astype(jnp.bfloat16)
        out[:, depth:] = resplit(value[:, depth:], experts)


def pair_sums(near, other, experts, count):
    rows, width = near.shape[0] // count, near.shape[1]
    return local_call(
        functools.partial(pair_kernel, experts=experts),
        "pair_sums",
        2,
        0,
        6 * near.size,
        [VMEM] * 2,
        [VMEM] * count,
        [shaped((rows, width))] * count,
    )(near, other)


def plane_kernel(*refs, experts, pieces):
    blocks, outs = refs[:-pieces], refs[-pieces:]
    width = outs[0].shape[1] - EXTRA
    depth = width * pieces

    def total(start, size):
        values = [b[:, start : start + size].astype(jnp.float32) for b in blocks]
        return functools.reduce(lambda a, b: a + b, values)

    extra = resplit(total(depth, EXTRA), experts)
    for k, out in enumerate(outs):
        out[:, :width] = total(k * width, width).astype(jnp.bfloat16)
        out[:, width:] = extra


def plane_sums(blocks, experts, pieces):
    rows, width = blocks[0].shape[0], (blocks[0].shape[1] - EXTRA) // pieces + EXTRA
    return local_call(
        functools.partial(plane_kernel, experts=experts, pieces=pieces),
        "plane_sums",
        2,
        0,
        2 * blocks[0].size * len(blocks),
        [VMEM] * len(blocks),
        [VMEM] * pieces,
        [shaped((rows, width))] * pieces,
    )(*blocks)


def tree_sum(parts):
    while len(parts) > 1:
        middle = len(parts) // 2
        parts = [a + b for a, b in zip(parts[:middle], parts[middle:], strict=True)]
    return parts[0]


def line_kernel(*refs, experts):
    blocks, (grads, routes) = refs[:-2], refs[-2:]
    width = grads.shape[1]
    grads[...] = tree_sum([b[:, :width].astype(jnp.float32) for b in blocks]).astype(jnp.bfloat16)
    extra = tree_sum([b[:, width:].astype(jnp.float32) for b in blocks])
    total = extra + pltpu.roll(extra, EXTRA - experts, 1)
    routes[...] = total.astype(jnp.bfloat16).astype(jnp.float32)


def line_sums(blocks, experts):
    rows, width = blocks[0].shape[0], blocks[0].shape[1] - EXTRA
    return local_call(
        functools.partial(line_kernel, experts=experts),
        "line_sums",
        2,
        0,
        2 * blocks[0].size * len(blocks),
        [VMEM] * len(blocks),
        [VMEM] * 2,
        [shaped((rows, width)), shaped((rows, EXTRA), jnp.float32)],
    )(*blocks)


def per_device(tokens_in, out_grad, route_ids, route_weight, gate_weight, up_weight, down_weight):
    experts = lax.axis_size("expert")
    seqs = lax.axis_size("seq")
    pieces = lax.axis_size("tensor")
    depth = tokens_in.shape[1] * pieces
    place = jnp.stack([lax.axis_index("tensor"), lax.axis_index("expert")]).astype(jnp.int32)
    chips = experts // 2
    planes = [(dx, ds) for ds in range(seqs) for dx in range(chips)]

    def along(value, shift):
        pairs = [(i, (i + shift) % pieces) for i in range(pieces)]
        return lax.ppermute(value, "tensor", pairs)

    def across(value, dx, ds):
        pairs = []
        for e in range(experts):
            for s in range(seqs):
                to_e = ((e // 2 + dx) % chips) * 2 + e % 2
                pairs.append((e * seqs + s, to_e * seqs + (s + ds) % seqs))
        return lax.ppermute(value, ("expert", "seq"), pairs)

    def swap(value):
        return lax.ppermute(value, "expert", [(e, e ^ 1) for e in range(experts)])

    expert_ids = jnp.arange(EXTRA, dtype=jnp.int32)
    chosen = (route_ids[:, :, None] == expert_ids[None, None, :]).astype(jnp.float32)
    weights = jnp.sum(chosen * route_weight.astype(jnp.float32)[:, :, None], axis=1)
    both = first_pair(tokens_in, out_grad)
    arrived = [along(both, k) for k in range(1, pieces)]
    early, late = range(pieces // 2), range(pieces // 2, pieces)
    turned_down = turned(place, pieces, down_weight, False, early)
    line_x, line_g = line_pair([both] + arrived, weights.astype(jnp.bfloat16), turned_down[0])
    from_x = [across(line_x, dx, ds) for dx, ds in planes[1:]]
    turned_gate = turned(place, pieces, gate_weight, True, range(pieces))
    turned_up = turned(place, pieces, up_weight, True, early)
    near_x = stacked([line_x] + from_x, 0, [turned_gate[0], turned_up[0]])
    far_x = swap(near_x)
    from_g = [across(line_g, dx, ds) for dx, ds in planes[1:]]
    turned_up = turned_up + turned(place, pieces, up_weight, True, late, [near_x])
    gate, up, weight = gate_up(place, near_x, far_x, turned_gate, turned_up)
    near_g = stacked([line_g] + from_g, 0, [weight])
    far_g = swap(near_g)
    turned_down = turned_down + turned(place, pieces, down_weight, False, late, [near_g])
    near_d, far_d, dgate, dup, hidw = middle(
        place, experts, pieces, near_g, far_g, weight, gate, up, turned_down, turned_gate, turned_up
    )

    other_d = swap(far_d)
    chunks = depth // chunk_of(depth // pieces)
    down_grad = down_grads(place, pieces, near_g, far_g, hidw, depth, 0, chunks // 2)
    gate_grad = columns_grad(place, pieces, near_x, far_x, dgate, depth)
    up_grad = columns_grad(place, pieces, near_x, far_x, dup, depth)
    down_grad = down_grads(
        place, pieces, near_g, far_g, hidw, depth, chunks // 2, chunks, [down_grad]
    )

    blocks = pair_sums(near_d, other_d, experts, len(planes))
    arrived = [
        across(block, -dx, -ds) for block, (dx, ds) in zip(blocks[1:], planes[1:], strict=True)
    ]
    sends = plane_sums([blocks[0]] + arrived, experts, pieces)
    finals = [sends[0]] + [along(sends[k], -k) for k in range(1, pieces)]
    x_grad, routes = line_sums(finals, experts)
    route_grad = jnp.sum(chosen * routes[:, None, :], axis=2).astype(jnp.bfloat16)
    return (x_grad, route_grad, gate_grad, up_grad, down_grad)


def solution(mesh):
    in_specs = (
        P(("expert", "seq"), "tensor"),
        P(("expert", "seq"), "tensor"),
        P(("expert", "seq"), None),
        P(("expert", "seq"), None),
        P("expert", None, ("seq", "tensor")),
        P("expert", None, ("seq", "tensor")),
        P("expert", ("seq", "tensor"), None),
    )
    out_specs = (
        P(("expert", "seq"), "tensor"),
        P(("expert", "seq"), None),
        P("expert", None, ("seq", "tensor")),
        P("expert", None, ("seq", "tensor")),
        P("expert", ("seq", "tensor"), None),
    )
    return jax.shard_map(
        per_device, mesh=mesh, in_specs=in_specs, out_specs=out_specs, check_vma=False
    )
```

```python
import functools

import jax
import jax.numpy as jnp
from jax import lax
from jax.experimental import pallas as pl
from jax.experimental.pallas import tpu as pltpu
from jax.sharding import PartitionSpec as P

EXTRA = 128
SLOTS = 6
TURN_CHUNK = 384
GRAD_CHUNK = 256
MIB = 1 << 20
PLAIN = (((1,), (0,)), ((), ()))
CONTRACT_ROWS = (((0,), (0,)), ((), ()))
CONTRACT_COLS = (((1,), (1,)), ((), ()))
VMEM = pl.BlockSpec(memory_space=pltpu.VMEM)
SMEM = pl.BlockSpec(memory_space=pltpu.SMEM)
ANY = pl.BlockSpec(memory_space=pl.ANY)
HBM = pl.BlockSpec(memory_space=pltpu.HBM)


def matmul(a, b, dims=PLAIN):
    return lax.dot_general(a, b, dims, preferred_element_type=jnp.float32)


def shaped(shape, dtype=jnp.bfloat16):
    return jax.ShapeDtypeStruct(shape, dtype)


def local_call(
    body, name, mib, flops, moved, in_specs, out_specs, out_shape, scratch=(), aliases=None
):
    return pl.pallas_call(
        body,
        in_specs=in_specs,
        out_specs=out_specs,
        out_shape=out_shape,
        scratch_shapes=list(scratch),
        input_output_aliases=aliases or {},
        compiler_params=pltpu.CompilerParams(vmem_limit_bytes=mib * MIB),
        cost_estimate=pl.CostEstimate(
            flops=int(flops), bytes_accessed=int(moved), transcendentals=0
        ),
        name=name,
    )


def chunk_of(features, most=768):
    for size in (768, 512, 384, 256, 128):
        if features % size == 0 and size <= most:
            return size
    return features


def whole_chunks(home, pieces, depth, most=768):
    width = depth // pieces
    size = chunk_of(width, most)
    found = []
    for k in range(pieces):
        owner = lax.rem(home - k + pieces, pieces)
        for c in range(width // size):
            start = pl.multiple_of(owner * width + c * size, size)
            found.append((k * width + c * size, start))
    return size, found


def both_rows(near, far, start, size):
    return jnp.concatenate([near[:, start : start + size], far[:, start : start + size]], axis=0)


def jobs_chunks(place, pieces, jobs, depth):
    width = depth // pieces
    size, chunks = whole_chunks(place[0], pieces, depth, TURN_CHUNK)
    found, base = [], 0
    for weight, by_rows, which in jobs:
        for rel, start in chunks:
            if rel // width in which:
                found.append((weight, by_rows, base + rel // width - which.start, rel % width, start))
        base += len(which)
    return size, found


def turn_into(out, base, value, by_rows):
    rows, columns = value.shape
    for at in range(0, columns, EXTRA):
        turned_part = value[:, at : at + EXTRA].T
        if by_rows:
            out[at : at + EXTRA, base : base + rows] = turned_part
        else:
            out[base + at : base + at + EXTRA, :] = turned_part


def turned_kernel(place, *refs, pieces, jobs, depth):
    weights = refs[: len(jobs)]
    count = sum(len(which) for _, _, which in jobs)
    *outs, flat, tall, sems = refs[-count - 3 :]
    jobs = [(w, by_rows, which) for w, (_, by_rows, which) in zip(weights, jobs, strict=True)]
    size, chunks = jobs_chunks(place, pieces, jobs, depth)

    def buffer(j):
        return (flat if chunks[j][1] else tall).at[j % SLOTS]

    def copy(j):
        weight, by_rows, _, _, start = chunks[j]
        span = pl.ds(start, size)
        source = weight.at[0, span] if by_rows else weight.at[0, :, span]
        return pltpu.make_async_copy(source, buffer(j), sems.at[j % SLOTS])

    for j in range(min(SLOTS, len(chunks))):
        copy(j).start()
    for j, (_, by_rows, out, base, _) in enumerate(chunks):
        copy(j).wait()
        turn_into(outs[out], base, buffer(j), by_rows)
        if j + SLOTS < len(chunks):
            copy(j + SLOTS).start()


def turned(place, pieces, jobs, depth, after=()):
    width = depth // pieces
    size = chunk_of(width, TURN_CHUNK)
    hidden = jobs[0][0].shape[2] if jobs[0][1] else jobs[0][0].shape[1]
    shapes = []
    for _, by_rows, which in jobs:
        shapes += [shaped((hidden, width) if by_rows else (width, hidden))] * len(which)
    kinds = {by_rows for _, by_rows, _ in jobs}
    weights = [pltpu.with_memory_space_constraint(w, pltpu.HBM) for w, _, _ in jobs]
    shared = functools.partial(
        turned_kernel, pieces=pieces, jobs=[(None, b, which) for _, b, which in jobs], depth=depth
    )
    found = local_call(
        shared,
        "turned",
        7 * len(kinds),
        0,
        0,
        [SMEM] + [HBM] * len(weights) + [ANY] * len(after),
        [VMEM] * len(shapes),
        shapes,
        [
            pltpu.VMEM((SLOTS if True in kinds else 1, size, hidden), jnp.bfloat16),
            pltpu.VMEM((SLOTS if False in kinds else 1, hidden, size), jnp.bfloat16),
            pltpu.SemaphoreType.DMA((SLOTS,)),
        ],
    )(place, *weights, *after)
    result, at = [], 0
    for _, _, which in jobs:
        result.append(found[at : at + len(which)])
        at += len(which)
    return result


def gate_up_kernel(place, xp, xo, wu, *refs, pieces):
    wg, refs = refs[:pieces], refs[pieces:]
    gate, up, weight, *outs, buf, sems = refs
    hidden, width = wg[0].shape
    size, chunks = whole_chunks(place[0], pieces, width * pieces, TURN_CHUNK)
    slots = buf.shape[0]

    def copy(j):
        span = pl.ds(chunks[j][1], size)
        return pltpu.make_async_copy(wu.at[0, span], buf.at[j % slots], sems.at[j % slots])

    for j in range(min(slots, len(chunks))):
        copy(j).start()
    for k, w in enumerate(wg):
        rows = both_rows(xp, xo, k * width, width)
        for at in range(0, hidden, EXTRA):
            value = matmul(rows, w[at : at + EXTRA, :], CONTRACT_COLS)
            if k == 0:
                gate[:, at : at + EXTRA] = value
            else:
                gate[:, at : at + EXTRA] += value
    lane = lax.broadcasted_iota(jnp.int32, (1, EXTRA), 1)
    mine = both_rows(xp, xo, width * pieces, EXTRA).astype(jnp.float32)
    total = jnp.sum(jnp.where(lane == place[1], mine, 0.0), axis=1, keepdims=True)
    weight[...] = jnp.broadcast_to(total, weight.shape)
    for j, (rel, _) in enumerate(chunks):
        copy(j).wait()
        piece = buf.at[j % slots]
        value = matmul(both_rows(xp, xo, rel, size), piece[...])
        if j == 0:
            up[...] = value
        else:
            up[...] += value
        turn_into(outs[rel // width], rel % width, piece, True)
        if j + slots < len(chunks):
            copy(j + slots).start()


def gate_up(place, near, far, turned_gate, w_up):
    half = near.shape[0]
    pieces = len(turned_gate)
    hidden, width = turned_gate[0].shape
    out = shaped((2 * half, hidden), jnp.float32)
    gate, up, weight, *turned_up = local_call(
        functools.partial(gate_up_kernel, pieces=pieces),
        "gate_up",
        10,
        0,
        0,
        [SMEM] + [VMEM] * 2 + [HBM] + [VMEM] * pieces,
        [VMEM] * (3 + pieces),
        [out, out, shaped((2 * half, EXTRA), jnp.float32)] + [shaped((hidden, width))] * pieces,
        [
            pltpu.VMEM((8, chunk_of(width, TURN_CHUNK), hidden), jnp.bfloat16),
            pltpu.SemaphoreType.DMA((8,)),
        ],
    )(place, near, far, pltpu.with_memory_space_constraint(w_up, pltpu.HBM), *turned_gate)
    return gate, up, weight, turned_up


def middle_kernel(
    place, gp, go, weight_in, gate, up, *refs, pieces, experts
):
    wd, wg, wu = refs[:pieces], refs[pieces : 2 * pieces], refs[2 * pieces : 3 * pieces]
    near, far, dgate, dup, hidw, raw = refs[3 * pieces :]
    width = wg[0].shape[1]
    half = near.shape[0]
    depth = width * pieces
    for k in range(pieces):
        value = matmul(both_rows(gp, go, k * width, width), wd[k][...])
        if k == 0:
            raw[...] = value
        else:
            raw[...] += value
    lane = lax.broadcasted_iota(jnp.int32, (1, EXTRA), 1)
    mine = lane == place[1]
    weight = weight_in[:, :1]
    gate_value = gate[...]
    up_value = up[...]
    raw_value = raw[...]
    sigmoid_gate = jax.nn.sigmoid(gate_value)
    activated = gate_value * sigmoid_gate
    hidden_value = activated * up_value
    scaled = weight * raw_value
    slope = sigmoid_gate * (1.0 + gate_value * (1.0 - sigmoid_gate))
    dgate[...] = (scaled * up_value * slope).astype(jnp.bfloat16)
    dup[...] = (scaled * activated).astype(jnp.bfloat16)
    hidw[...] = (weight * hidden_value).astype(jnp.bfloat16)
    total = jnp.sum(hidden_value * raw_value, axis=1, keepdims=True)
    high = total.astype(jnp.bfloat16).astype(jnp.float32)
    low = total - high
    placed = jnp.where(mine, high, 0.0) + jnp.where(lane == place[1] + experts, low, 0.0)
    placed = placed.astype(jnp.bfloat16)
    near[:, depth:] = placed[:half]
    far[:, depth:] = placed[half:]
    step = chunk_of(width)
    for at in range(0, depth, step):
        k, base = at // width, at % width
        span = slice(base, base + step)
        value = matmul(dgate[...], wg[k][:, span]) + matmul(dup[...], wu[k][:, span])
        value = value.astype(jnp.bfloat16)
        near[:, at : at + step] = value[:half]
        far[:, at : at + step] = value[half:]


def middle(place, experts, pieces, near, far, weight, gate, up, turned_down, turned_gate, turned_up):
    half = near.shape[0]
    hidden, width = turned_gate[0].shape
    depth = width * pieces
    out = shaped((2 * half, hidden))
    result = shaped((half, depth + EXTRA))
    return local_call(
        functools.partial(middle_kernel, pieces=pieces, experts=experts),
        "middle",
        4,
        0,
        0,
        [SMEM] + [VMEM] * (5 + 3 * pieces),
        [VMEM] * 5,
        [result, result, out, out, out],
        [pltpu.VMEM((2 * half, hidden), jnp.float32)],
    )(place, near, far, weight, gate, up, *turned_down, *turned_gate, *turned_up)


def weight_kernel(place, near, far, *refs, pieces, jobs, by_rows):
    deltas = refs[: len(jobs)]
    *outs, buf, sems = refs[-len(jobs) - 2 :]
    depth = outs[0].shape[1] if by_rows else outs[0].shape[2]
    size, chunks = whole_chunks(place[0], pieces, depth, GRAD_CHUNK)
    copies = []
    for delta, out, (first, last) in zip(deltas, outs, jobs, strict=True):
        for rel, start in chunks[first:last]:
            j = len(copies)
            rows = both_rows(near, far, rel, size)
            span = pl.ds(start, size)
            if by_rows:
                value, target = matmul(rows, delta[...], CONTRACT_ROWS), out.at[0, span]
            else:
                value, target = matmul(delta[...], rows, CONTRACT_ROWS), out.at[0, :, span]
            buf[j] = value.astype(jnp.bfloat16)
            copy = pltpu.make_async_copy(buf.at[j], target, sems.at[j])
            copy.start()
            copies.append(copy)
    for copy in copies:
        copy.wait()


def weight_grads(place, pieces, near, far, depth, by_rows, jobs):
    half = near.shape[0]
    hidden = jobs[0][0].shape[1]
    size = chunk_of(depth // pieces, GRAD_CHUNK)
    count = sum(last - first for _, first, last, _ in jobs)
    there = [(i, job[3]) for i, job in enumerate(jobs) if job[3] is not None]
    held = [pltpu.with_memory_space_constraint(g, pltpu.HBM) for _, g in there]
    return local_call(
        functools.partial(
            weight_kernel, pieces=pieces, jobs=[job[1:3] for job in jobs], by_rows=by_rows
        ),
        "weight_grads",
        4 + (count * size * hidden * 2) // MIB,
        4 * half * size * count * hidden,
        2 * size * count * hidden,
        [SMEM] + [VMEM] * (2 + len(jobs)) + [HBM] * len(held),
        [ANY] * len(jobs),
        [shaped((1, depth, hidden) if by_rows else (1, hidden, depth))] * len(jobs),
        [
            pltpu.VMEM((count, size, hidden) if by_rows else (count, hidden, size), jnp.bfloat16),
            pltpu.SemaphoreType.DMA((count,)),
        ],
        aliases={3 + len(jobs) + n: i for n, (i, _) in enumerate(there)},
    )(place, near, far, *[job[0] for job in jobs], *held)


def stack_kernel(*refs, axis, count):
    out = refs[-1]
    at = 0
    for ref in refs[:count]:
        size = ref.shape[axis]
        if axis:
            out[:, at : at + size] = ref[...]
        else:
            out[at : at + size, :] = ref[...]
        at += size


def stacked(blocks, axis, after=()):
    shape = list(blocks[0].shape)
    shape[axis] = sum(b.shape[axis] for b in blocks)
    count = shape[0] * shape[1]
    return local_call(
        functools.partial(stack_kernel, axis=axis, count=len(blocks)),
        "stacked",
        2,
        0,
        4 * count,
        [VMEM] * len(blocks) + [ANY] * len(after),
        VMEM,
        shaped(tuple(shape)),
    )(*blocks, *after)


def first_kernel(x, g, out, sems):
    rows = x.shape[0]
    copies = [
        pltpu.make_async_copy(ref, out.at[pl.ds(i * rows, rows)], sems.at[i])
        for i, ref in enumerate((x, g))
    ]
    for copy in copies:
        copy.start()
    for copy in copies:
        copy.wait()


def first_pair(x, g):
    rows, width = x.shape
    return local_call(
        first_kernel,
        "first_pair",
        1,
        0,
        8 * rows * width,
        [HBM] * 2,
        VMEM,
        shaped((2 * rows, width)),
        [pltpu.SemaphoreType.DMA((2,))],
    )(*(pltpu.with_memory_space_constraint(v, pltpu.HBM) for v in (x, g)))


def line_pair_kernel(*refs):
    *blocks, extra, _, line_x, line_g = refs
    rows = line_x.shape[0]
    width = blocks[0].shape[1]
    for k, block in enumerate(blocks):
        line_x[:, k * width : (k + 1) * width] = block[:rows, :]
        line_g[:, k * width : (k + 1) * width] = block[rows:, :]
    line_x[:, len(blocks) * width :] = extra[...]


def line_pair(blocks, extra, after):
    rows = extra.shape[0]
    depth = blocks[0].shape[1] * len(blocks)
    return local_call(
        line_pair_kernel,
        "line_pair",
        2,
        0,
        8 * rows * depth,
        [VMEM] * (len(blocks) + 1) + [ANY],
        [VMEM] * 2,
        [shaped((rows, depth + EXTRA)), shaped((rows, depth))],
    )(*blocks, extra, after)


def resplit(extra, experts):
    lane = lax.broadcasted_iota(jnp.int32, extra.shape, 1)
    total = extra + pltpu.roll(extra, EXTRA - experts, 1)
    total = jnp.where(lane < experts, total, 0.0)
    high = total.astype(jnp.bfloat16).astype(jnp.float32)
    return (high + pltpu.roll(total - high, experts, 1)).astype(jnp.bfloat16)


def pair_kernel(near, other, *outs, experts):
    rows, width = outs[0].shape
    depth = width - EXTRA
    for i, out in enumerate(outs):
        span = pl.ds(i * rows, rows)
        value = near[span, :].astype(jnp.float32) + other[span, :].astype(jnp.float32)
        out[:, :depth] = value[:, :depth].astype(jnp.bfloat16)
        out[:, depth:] = resplit(value[:, depth:], experts)


def pair_sums(near, other, experts, count):
    rows, width = near.shape[0] // count, near.shape[1]
    return local_call(
        functools.partial(pair_kernel, experts=experts),
        "pair_sums",
        2,
        0,
        6 * near.size,
        [VMEM] * 2,
        [VMEM] * count,
        [shaped((rows, width))] * count,
    )(near, other)


def plane_kernel(*refs, experts, pieces):
    blocks, outs = refs[:-pieces], refs[-pieces:]
    width = outs[0].shape[1] - EXTRA
    depth = width * pieces

    def total(start, size):
        values = [b[:, start : start + size].astype(jnp.float32) for b in blocks]
        return functools.reduce(lambda a, b: a + b, values)

    extra = resplit(total(depth, EXTRA), experts)
    for k, out in enumerate(outs):
        out[:, :width] = total(k * width, width).astype(jnp.bfloat16)
        out[:, width:] = extra


def plane_sums(blocks, experts, pieces):
    rows, width = blocks[0].shape[0], (blocks[0].shape[1] - EXTRA) // pieces + EXTRA
    return local_call(
        functools.partial(plane_kernel, experts=experts, pieces=pieces),
        "plane_sums",
        2,
        0,
        2 * blocks[0].size * len(blocks),
        [VMEM] * len(blocks),
        [VMEM] * pieces,
        [shaped((rows, width))] * pieces,
    )(*blocks)


def tree_sum(parts):
    while len(parts) > 1:
        middle = len(parts) // 2
        parts = [a + b for a, b in zip(parts[:middle], parts[middle:], strict=True)]
    return parts[0]


def line_kernel(*refs, experts):
    blocks, (grads, routes) = refs[:-2], refs[-2:]
    width = grads.shape[1]
    grads[...] = tree_sum([b[:, :width].astype(jnp.float32) for b in blocks]).astype(jnp.bfloat16)
    extra = tree_sum([b[:, width:].astype(jnp.float32) for b in blocks])
    total = extra + pltpu.roll(extra, EXTRA - experts, 1)
    routes[...] = total.astype(jnp.bfloat16).astype(jnp.float32)


def line_sums(blocks, experts):
    rows, width = blocks[0].shape[0], blocks[0].shape[1] - EXTRA
    return local_call(
        functools.partial(line_kernel, experts=experts),
        "line_sums",
        2,
        0,
        2 * blocks[0].size * len(blocks),
        [VMEM] * len(blocks),
        [VMEM] * 2,
        [shaped((rows, width)), shaped((rows, EXTRA), jnp.float32)],
    )(*blocks)


def per_device(tokens_in, out_grad, route_ids, route_weight, gate_weight, up_weight, down_weight):
    experts = lax.axis_size("expert")
    seqs = lax.axis_size("seq")
    pieces = lax.axis_size("tensor")
    depth = tokens_in.shape[1] * pieces
    place = jnp.stack([lax.axis_index("tensor"), lax.axis_index("expert")]).astype(jnp.int32)
    chips = experts // 2
    planes = [(dx, ds) for ds in range(seqs) for dx in range(chips)]

    def along(value, shift):
        pairs = [(i, (i + shift) % pieces) for i in range(pieces)]
        return lax.ppermute(value, "tensor", pairs)

    def across(value, dx, ds):
        pairs = []
        for e in range(experts):
            for s in range(seqs):
                to_e = ((e // 2 + dx) % chips) * 2 + e % 2
                pairs.append((e * seqs + s, to_e * seqs + (s + ds) % seqs))
        return lax.ppermute(value, ("expert", "seq"), pairs)

    def swap(value):
        return lax.ppermute(value, "expert", [(e, e ^ 1) for e in range(experts)])

    expert_ids = jnp.arange(EXTRA, dtype=jnp.int32)
    chosen = (route_ids[:, :, None] == expert_ids[None, None, :]).astype(jnp.float32)
    weights = jnp.sum(chosen * route_weight.astype(jnp.float32)[:, :, None], axis=1)
    both = first_pair(tokens_in, out_grad)
    arrived = [along(both, k) for k in range(1, pieces)]
    everything = range(pieces)
    early, late = range(pieces // 2), range(pieces // 2, pieces)
    (turned_down,) = turned(place, pieces, [(down_weight, False, early)], depth)
    line_x, line_g = line_pair([both] + arrived, weights.astype(jnp.bfloat16), turned_down[0])
    from_x = [across(line_x, dx, ds) for dx, ds in planes[1:]]
    turned_gate, more_down = turned(
        place, pieces, [(gate_weight, True, everything), (down_weight, False, late)], depth
    )
    near_x = stacked([line_x] + from_x, 0, [turned_gate[0]])
    far_x = swap(near_x)
    from_g = [across(line_g, dx, ds) for dx, ds in planes[1:]]
    gate, up, weight, turned_up = gate_up(place, near_x, far_x, turned_gate, up_weight)
    near_g = stacked([line_g] + from_g, 0, [weight])
    far_g = swap(near_g)
    near_d, far_d, dgate, dup, hidw = middle(
        place, experts, pieces, near_g, far_g, weight, gate, up,
        turned_down + more_down, turned_gate, turned_up,
    )

    other_d = swap(far_d)
    chunks = depth // chunk_of(depth // pieces, GRAD_CHUNK)
    some = chunks // 3
    (gate_grad,) = weight_grads(place, pieces, near_x, far_x, depth, True, [(dgate, 0, some, None)])
    gate_grad, up_grad = weight_grads(
        place, pieces, near_x, far_x, depth, True,
        [(dgate, some, chunks, gate_grad), (dup, 0, chunks, None)],
    )
    (down_grad,) = weight_grads(
        place, pieces, near_g, far_g, depth, False, [(hidw, 0, chunks, None)]
    )

    blocks = pair_sums(near_d, other_d, experts, len(planes))
    arrived = [
        across(block, -dx, -ds) for block, (dx, ds) in zip(blocks[1:], planes[1:], strict=True)
    ]
    sends = plane_sums([blocks[0]] + arrived, experts, pieces)
    finals = [sends[0]] + [along(sends[k], -k) for k in range(1, pieces)]
    x_grad, routes = line_sums(finals, experts)
    route_grad = jnp.sum(chosen * routes[:, None, :], axis=2).astype(jnp.bfloat16)
    return (x_grad, route_grad, gate_grad, up_grad, down_grad)


def solution(mesh):
    in_specs = (
        P(("expert", "seq"), "tensor"),
        P(("expert", "seq"), "tensor"),
        P(("expert", "seq"), None),
        P(("expert", "seq"), None),
        P("expert", None, ("seq", "tensor")),
        P("expert", None, ("seq", "tensor")),
        P("expert", ("seq", "tensor"), None),
    )
    out_specs = (
        P(("expert", "seq"), "tensor"),
        P(("expert", "seq"), None),
        P("expert", None, ("seq", "tensor")),
        P("expert", None, ("seq", "tensor")),
        P("expert", ("seq", "tensor"), None),
    )
    return jax.shard_map(
        per_device, mesh=mesh, in_specs=in_specs, out_specs=out_specs, check_vma=False
    )
```

```python
import functools

import jax
import jax.numpy as jnp
from jax import lax
from jax.experimental import pallas as pl
from jax.experimental.pallas import tpu as pltpu
from jax.sharding import PartitionSpec as P

EXTRA = 128
SLOTS = 6
TURN_CHUNK = 384
GRAD_CHUNK = 256
MIB = 1 << 20
PLAIN = (((1,), (0,)), ((), ()))
CONTRACT_ROWS = (((0,), (0,)), ((), ()))
CONTRACT_COLS = (((1,), (1,)), ((), ()))
VMEM = pl.BlockSpec(memory_space=pltpu.VMEM)
SMEM = pl.BlockSpec(memory_space=pltpu.SMEM)
ANY = pl.BlockSpec(memory_space=pl.ANY)
HBM = pl.BlockSpec(memory_space=pltpu.HBM)


def matmul(a, b, dims=PLAIN):
    return lax.dot_general(a, b, dims, preferred_element_type=jnp.float32)


def shaped(shape, dtype=jnp.bfloat16):
    return jax.ShapeDtypeStruct(shape, dtype)


def local_call(
    body, name, mib, flops, moved, in_specs, out_specs, out_shape, scratch=(), aliases=None
):
    return pl.pallas_call(
        body,
        in_specs=in_specs,
        out_specs=out_specs,
        out_shape=out_shape,
        scratch_shapes=list(scratch),
        input_output_aliases=aliases or {},
        compiler_params=pltpu.CompilerParams(vmem_limit_bytes=mib * MIB),
        cost_estimate=pl.CostEstimate(
            flops=int(flops), bytes_accessed=int(moved), transcendentals=0
        ),
        name=name,
    )


def chunk_of(features, most=768):
    for size in (768, 512, 384, 256, 128):
        if features % size == 0 and size <= most:
            return size
    return features


def whole_chunks(home, pieces, depth, most=768):
    width = depth // pieces
    size = chunk_of(width, most)
    found = []
    for k in range(pieces):
        owner = lax.rem(home - k + pieces, pieces)
        for c in range(width // size):
            start = pl.multiple_of(owner * width + c * size, size)
            found.append((k * width + c * size, start))
    return size, found


def both_rows(near, far, start, size):
    return jnp.concatenate([near[:, start : start + size], far[:, start : start + size]], axis=0)


def jobs_chunks(place, pieces, jobs, depth):
    width = depth // pieces
    size, chunks = whole_chunks(place[0], pieces, depth, TURN_CHUNK)
    found, base = [], 0
    for weight, by_rows, which in jobs:
        for rel, start in chunks:
            if rel // width in which:
                found.append((weight, by_rows, base + rel // width - which.start, rel % width, start))
        base += len(which)
    return size, found


def turn_into(out, base, value, by_rows):
    rows, columns = value.shape
    for at in range(0, columns, EXTRA):
        turned_part = value[:, at : at + EXTRA].T
        if by_rows:
            out[at : at + EXTRA, base : base + rows] = turned_part
        else:
            out[base + at : base + at + EXTRA, :] = turned_part


def turned_kernel(place, *refs, pieces, jobs, depth):
    weights = refs[: len(jobs)]
    count = sum(len(which) for _, _, which in jobs)
    *outs, flat, tall, sems = refs[-count - 3 :]
    jobs = [(w, by_rows, which) for w, (_, by_rows, which) in zip(weights, jobs, strict=True)]
    size, chunks = jobs_chunks(place, pieces, jobs, depth)

    def buffer(j):
        return (flat if chunks[j][1] else tall).at[j % SLOTS]

    def copy(j):
        weight, by_rows, _, _, start = chunks[j]
        span = pl.ds(start, size)
        source = weight.at[0, span] if by_rows else weight.at[0, :, span]
        return pltpu.make_async_copy(source, buffer(j), sems.at[j % SLOTS])

    for j in range(min(SLOTS, len(chunks))):
        copy(j).start()
    for j, (_, by_rows, out, base, _) in enumerate(chunks):
        copy(j).wait()
        turn_into(outs[out], base, buffer(j), by_rows)
        if j + SLOTS < len(chunks):
            copy(j + SLOTS).start()


def turned(place, pieces, jobs, depth, after=()):
    width = depth // pieces
    size = chunk_of(width, TURN_CHUNK)
    hidden = jobs[0][0].shape[2] if jobs[0][1] else jobs[0][0].shape[1]
    shapes = []
    for _, by_rows, which in jobs:
        shapes += [shaped((hidden, width) if by_rows else (width, hidden))] * len(which)
    kinds = {by_rows for _, by_rows, _ in jobs}
    weights = [pltpu.with_memory_space_constraint(w, pltpu.HBM) for w, _, _ in jobs]
    shared = functools.partial(
        turned_kernel, pieces=pieces, jobs=[(None, b, which) for _, b, which in jobs], depth=depth
    )
    found = local_call(
        shared,
        "turned",
        7 * len(kinds),
        0,
        0,
        [SMEM] + [HBM] * len(weights) + [ANY] * len(after),
        [VMEM] * len(shapes),
        shapes,
        [
            pltpu.VMEM((SLOTS if True in kinds else 1, size, hidden), jnp.bfloat16),
            pltpu.VMEM((SLOTS if False in kinds else 1, hidden, size), jnp.bfloat16),
            pltpu.SemaphoreType.DMA((SLOTS,)),
        ],
    )(place, *weights, *after)
    result, at = [], 0
    for _, _, which in jobs:
        result.append(found[at : at + len(which)])
        at += len(which)
    return result


def gate_up_kernel(place, xp, xo, wu, *refs, pieces):
    wg, refs = refs[:pieces], refs[pieces:]
    gate, up, weight, *outs, buf, sems = refs
    hidden, width = wg[0].shape
    size, chunks = whole_chunks(place[0], pieces, width * pieces, TURN_CHUNK)
    slots = buf.shape[0]

    def copy(j):
        span = pl.ds(chunks[j][1], size)
        return pltpu.make_async_copy(wu.at[0, span], buf.at[j % slots], sems.at[j % slots])

    for j in range(min(slots, len(chunks))):
        copy(j).start()
    for k, w in enumerate(wg):
        rows = both_rows(xp, xo, k * width, width)
        for at in range(0, hidden, EXTRA):
            value = matmul(rows, w[at : at + EXTRA, :], CONTRACT_COLS)
            if k == 0:
                gate[:, at : at + EXTRA] = value
            else:
                gate[:, at : at + EXTRA] += value
    lane = lax.broadcasted_iota(jnp.int32, (1, EXTRA), 1)
    mine = both_rows(xp, xo, width * pieces, EXTRA).astype(jnp.float32)
    total = jnp.sum(jnp.where(lane == place[1], mine, 0.0), axis=1, keepdims=True)
    weight[...] = jnp.broadcast_to(total, weight.shape)
    for j, (rel, _) in enumerate(chunks):
        copy(j).wait()
        piece = buf.at[j % slots]
        value = matmul(both_rows(xp, xo, rel, size), piece[...])
        if j == 0:
            up[...] = value
        else:
            up[...] += value
        turn_into(outs[rel // width], rel % width, piece, True)
        if j + slots < len(chunks):
            copy(j + slots).start()


def gate_up(place, near, far, turned_gate, w_up):
    half = near.shape[0]
    pieces = len(turned_gate)
    hidden, width = turned_gate[0].shape
    out = shaped((2 * half, hidden), jnp.float32)
    gate, up, weight, *turned_up = local_call(
        functools.partial(gate_up_kernel, pieces=pieces),
        "gate_up",
        10,
        0,
        0,
        [SMEM] + [VMEM] * 2 + [HBM] + [VMEM] * pieces,
        [VMEM] * (3 + pieces),
        [out, out, shaped((2 * half, EXTRA), jnp.float32)] + [shaped((hidden, width))] * pieces,
        [
            pltpu.VMEM((8, chunk_of(width, TURN_CHUNK), hidden), jnp.bfloat16),
            pltpu.SemaphoreType.DMA((8,)),
        ],
    )(place, near, far, pltpu.with_memory_space_constraint(w_up, pltpu.HBM), *turned_gate)
    return gate, up, weight, turned_up


def middle_kernel(
    place, gp, go, weight_in, gate, up, *refs, pieces, experts
):
    wd, wg, wu = refs[:pieces], refs[pieces : 2 * pieces], refs[2 * pieces : 3 * pieces]
    near, far, dgate, dup, hidw, raw = refs[3 * pieces :]
    width = wg[0].shape[1]
    half = near.shape[0]
    depth = width * pieces
    for k in range(pieces):
        value = matmul(both_rows(gp, go, k * width, width), wd[k][...])
        if k == 0:
            raw[...] = value
        else:
            raw[...] += value
    lane = lax.broadcasted_iota(jnp.int32, (1, EXTRA), 1)
    mine = lane == place[1]
    weight = weight_in[:, :1]
    gate_value = gate[...]
    up_value = up[...]
    raw_value = raw[...]
    sigmoid_gate = jax.nn.sigmoid(gate_value)
    activated = gate_value * sigmoid_gate
    hidden_value = activated * up_value
    scaled = weight * raw_value
    slope = sigmoid_gate * (1.0 + gate_value * (1.0 - sigmoid_gate))
    dgate[...] = (scaled * up_value * slope).astype(jnp.bfloat16)
    dup[...] = (scaled * activated).astype(jnp.bfloat16)
    hidw[...] = (weight * hidden_value).astype(jnp.bfloat16)
    total = jnp.sum(hidden_value * raw_value, axis=1, keepdims=True)
    high = total.astype(jnp.bfloat16).astype(jnp.float32)
    low = total - high
    placed = jnp.where(mine, high, 0.0) + jnp.where(lane == place[1] + experts, low, 0.0)
    placed = placed.astype(jnp.bfloat16)
    near[:, depth:] = placed[:half]
    far[:, depth:] = placed[half:]
    step = chunk_of(width)
    for at in range(0, depth, step):
        k, base = at // width, at % width
        span = slice(base, base + step)
        value = matmul(dgate[...], wg[k][:, span]) + matmul(dup[...], wu[k][:, span])
        value = value.astype(jnp.bfloat16)
        near[:, at : at + step] = value[:half]
        far[:, at : at + step] = value[half:]


def middle(place, experts, pieces, near, far, weight, gate, up, turned_down, turned_gate, turned_up):
    half = near.shape[0]
    hidden, width = turned_gate[0].shape
    depth = width * pieces
    out = shaped((2 * half, hidden))
    result = shaped((half, depth + EXTRA))
    return local_call(
        functools.partial(middle_kernel, pieces=pieces, experts=experts),
        "middle",
        4,
        0,
        0,
        [SMEM] + [VMEM] * (5 + 3 * pieces),
        [VMEM] * 5,
        [result, result, out, out, out],
        [pltpu.VMEM((2 * half, hidden), jnp.float32)],
    )(place, near, far, weight, gate, up, *turned_down, *turned_gate, *turned_up)


def weight_kernel(place, near, far, *refs, pieces, jobs, by_rows):
    deltas = refs[: len(jobs)]
    *outs, buf, sems = refs[-len(jobs) - 2 :]
    depth = outs[0].shape[1] if by_rows else outs[0].shape[2]
    size, chunks = whole_chunks(place[0], pieces, depth, GRAD_CHUNK)
    copies = []
    for delta, out, (first, last) in zip(deltas, outs, jobs, strict=True):
        for rel, start in chunks[first:last]:
            j = len(copies)
            rows = both_rows(near, far, rel, size)
            span = pl.ds(start, size)
            if by_rows:
                value, target = matmul(rows, delta[...], CONTRACT_ROWS), out.at[0, span]
            else:
                value, target = matmul(delta[...], rows, CONTRACT_ROWS), out.at[0, :, span]
            buf[j] = value.astype(jnp.bfloat16)
            copy = pltpu.make_async_copy(buf.at[j], target, sems.at[j])
            copy.start()
            copies.append(copy)
    for copy in copies:
        copy.wait()


def weight_grads(place, pieces, near, far, depth, by_rows, jobs):
    half = near.shape[0]
    hidden = jobs[0][0].shape[1]
    size = chunk_of(depth // pieces, GRAD_CHUNK)
    count = sum(last - first for _, first, last, _ in jobs)
    there = [(i, job[3]) for i, job in enumerate(jobs) if job[3] is not None]
    held = [pltpu.with_memory_space_constraint(g, pltpu.HBM) for _, g in there]
    return local_call(
        functools.partial(
            weight_kernel, pieces=pieces, jobs=[job[1:3] for job in jobs], by_rows=by_rows
        ),
        "weight_grads",
        4 + (count * size * hidden * 2) // MIB,
        4 * half * size * count * hidden,
        2 * size * count * hidden,
        [SMEM] + [VMEM] * (2 + len(jobs)) + [HBM] * len(held),
        [ANY] * len(jobs),
        [shaped((1, depth, hidden) if by_rows else (1, hidden, depth))] * len(jobs),
        [
            pltpu.VMEM((count, size, hidden) if by_rows else (count, hidden, size), jnp.bfloat16),
            pltpu.SemaphoreType.DMA((count,)),
        ],
        aliases={3 + len(jobs) + n: i for n, (i, _) in enumerate(there)},
    )(place, near, far, *[job[0] for job in jobs], *held)


def stack_kernel(*refs, axis, count):
    out = refs[-1]
    at = 0
    for ref in refs[:count]:
        size = ref.shape[axis]
        if axis:
            out[:, at : at + size] = ref[...]
        else:
            out[at : at + size, :] = ref[...]
        at += size


def stacked(blocks, axis, after=()):
    shape = list(blocks[0].shape)
    shape[axis] = sum(b.shape[axis] for b in blocks)
    count = shape[0] * shape[1]
    return local_call(
        functools.partial(stack_kernel, axis=axis, count=len(blocks)),
        "stacked",
        2,
        0,
        4 * count,
        [VMEM] * len(blocks) + [ANY] * len(after),
        VMEM,
        shaped(tuple(shape)),
    )(*blocks, *after)


def first_kernel(x, g, out, sems):
    rows = x.shape[0]
    copies = [
        pltpu.make_async_copy(ref, out.at[pl.ds(i * rows, rows)], sems.at[i])
        for i, ref in enumerate((x, g))
    ]
    for copy in copies:
        copy.start()
    for copy in copies:
        copy.wait()


def first_pair(x, g):
    rows, width = x.shape
    return local_call(
        first_kernel,
        "first_pair",
        1,
        0,
        8 * rows * width,
        [HBM] * 2,
        VMEM,
        shaped((2 * rows, width)),
        [pltpu.SemaphoreType.DMA((2,))],
    )(*(pltpu.with_memory_space_constraint(v, pltpu.HBM) for v in (x, g)))


def token_columns(table, ids, weights):
    choices, rows = ids.shape
    table[...] = jnp.zeros_like(table)
    table[:choices, :rows] = ids[...].astype(jnp.float32)
    if weights is not None:
        table[choices : 2 * choices, :rows] = weights[...].astype(jnp.float32)
    return table[...].T[:rows]


def line_pair_kernel(*refs):
    *blocks, ids, weights, _, line_x, line_g, table = refs
    rows = line_x.shape[0]
    width = blocks[0].shape[1]
    for k, block in enumerate(blocks):
        line_x[:, k * width : (k + 1) * width] = block[:rows, :]
        line_g[:, k * width : (k + 1) * width] = block[rows:, :]
    choices = ids.shape[0]
    columns = token_columns(table, ids, weights)
    lane = lax.broadcasted_iota(jnp.int32, (rows, EXTRA), 1).astype(jnp.float32)
    extra = jnp.zeros((rows, EXTRA), jnp.float32)
    for k in range(choices):
        hit = lane == columns[:, k : k + 1]
        extra += jnp.where(hit, columns[:, choices + k : choices + k + 1], 0.0)
    line_x[:, len(blocks) * width :] = extra.astype(jnp.bfloat16)


def line_pair(blocks, ids, weights, after):
    rows = ids.shape[1]
    depth = blocks[0].shape[1] * len(blocks)
    return local_call(
        line_pair_kernel,
        "line_pair",
        2,
        0,
        8 * rows * depth,
        [VMEM] * (len(blocks) + 2) + [ANY],
        [VMEM] * 2,
        [shaped((rows, depth + EXTRA)), shaped((rows, depth))],
        [pltpu.VMEM((8, EXTRA), jnp.float32)],
    )(*blocks, ids, weights, after)


def resplit(extra, experts):
    lane = lax.broadcasted_iota(jnp.int32, extra.shape, 1)
    total = extra + pltpu.roll(extra, EXTRA - experts, 1)
    total = jnp.where(lane < experts, total, 0.0)
    high = total.astype(jnp.bfloat16).astype(jnp.float32)
    return (high + pltpu.roll(total - high, experts, 1)).astype(jnp.bfloat16)


def pair_kernel(near, other, *outs, experts):
    rows, width = outs[0].shape
    depth = width - EXTRA
    for i, out in enumerate(outs):
        span = pl.ds(i * rows, rows)
        value = near[span, :].astype(jnp.float32) + other[span, :].astype(jnp.float32)
        out[:, :depth] = value[:, :depth].astype(jnp.bfloat16)
        out[:, depth:] = resplit(value[:, depth:], experts)


def pair_sums(near, other, experts, count):
    rows, width = near.shape[0] // count, near.shape[1]
    return local_call(
        functools.partial(pair_kernel, experts=experts),
        "pair_sums",
        2,
        0,
        6 * near.size,
        [VMEM] * 2,
        [VMEM] * count,
        [shaped((rows, width))] * count,
    )(near, other)


def plane_kernel(*refs, experts, pieces):
    blocks, outs = refs[:-pieces], refs[-pieces:]
    width = outs[0].shape[1] - EXTRA
    depth = width * pieces

    def total(start, size):
        values = [b[:, start : start + size].astype(jnp.float32) for b in blocks]
        return functools.reduce(lambda a, b: a + b, values)

    extra = resplit(total(depth, EXTRA), experts)
    for k, out in enumerate(outs):
        out[:, :width] = total(k * width, width).astype(jnp.bfloat16)
        out[:, width:] = extra


def plane_sums(blocks, experts, pieces):
    rows, width = blocks[0].shape[0], (blocks[0].shape[1] - EXTRA) // pieces + EXTRA
    return local_call(
        functools.partial(plane_kernel, experts=experts, pieces=pieces),
        "plane_sums",
        2,
        0,
        2 * blocks[0].size * len(blocks),
        [VMEM] * len(blocks),
        [VMEM] * pieces,
        [shaped((rows, width))] * pieces,
    )(*blocks)


def tree_sum(parts):
    while len(parts) > 1:
        middle = len(parts) // 2
        parts = [a + b for a, b in zip(parts[:middle], parts[middle:], strict=True)]
    return parts[0]


def line_kernel(*refs, experts):
    *blocks, ids, grads, routes, table = refs
    rows, width = grads.shape
    grads[...] = tree_sum([b[:, :width].astype(jnp.float32) for b in blocks]).astype(jnp.bfloat16)
    extra = tree_sum([b[:, width:].astype(jnp.float32) for b in blocks])
    total = extra + pltpu.roll(extra, EXTRA - experts, 1)
    total = total.astype(jnp.bfloat16).astype(jnp.float32)
    columns = token_columns(table, ids, None)
    lane = lax.broadcasted_iota(jnp.int32, (rows, EXTRA), 1)
    chosen = jnp.zeros((rows, EXTRA), jnp.float32)
    for k in range(ids.shape[0]):
        hit = lane.astype(jnp.float32) == columns[:, k : k + 1]
        value = jnp.sum(jnp.where(hit, total, 0.0), axis=1, keepdims=True)
        chosen += jnp.where(lane == k, value, 0.0)
    routes[...] = chosen.T[: ids.shape[0], :].astype(jnp.bfloat16)


def line_sums(blocks, ids, experts):
    rows, width = blocks[0].shape[0], blocks[0].shape[1] - EXTRA
    return local_call(
        functools.partial(line_kernel, experts=experts),
        "line_sums",
        2,
        0,
        2 * blocks[0].size * len(blocks),
        [VMEM] * (len(blocks) + 1),
        [VMEM] * 2,
        [shaped((rows, width)), shaped(ids.shape)],
        [pltpu.VMEM((8, EXTRA), jnp.float32)],
    )(*blocks, ids)


def per_device(tokens_in, out_grad, route_ids, route_weight, gate_weight, up_weight, down_weight):
    experts = lax.axis_size("expert")
    seqs = lax.axis_size("seq")
    pieces = lax.axis_size("tensor")
    depth = tokens_in.shape[1] * pieces
    place = jnp.stack([lax.axis_index("tensor"), lax.axis_index("expert")]).astype(jnp.int32)
    chips = experts // 2
    planes = [(dx, ds) for ds in range(seqs) for dx in range(chips)]

    def along(value, shift):
        pairs = [(i, (i + shift) % pieces) for i in range(pieces)]
        return lax.ppermute(value, "tensor", pairs)

    def across(value, dx, ds):
        pairs = []
        for e in range(experts):
            for s in range(seqs):
                to_e = ((e // 2 + dx) % chips) * 2 + e % 2
                pairs.append((e * seqs + s, to_e * seqs + (s + ds) % seqs))
        return lax.ppermute(value, ("expert", "seq"), pairs)

    def swap(value):
        return lax.ppermute(value, "expert", [(e, e ^ 1) for e in range(experts)])

    ids, choice_weights = route_ids.T, route_weight.T
    both = first_pair(tokens_in, out_grad)
    arrived = [along(both, k) for k in range(1, pieces)]
    everything = range(pieces)
    early, late = range(pieces // 2), range(pieces // 2, pieces)
    (turned_down,) = turned(place, pieces, [(down_weight, False, early)], depth)
    line_x, line_g = line_pair([both] + arrived, ids, choice_weights, turned_down[0])
    from_x = [across(line_x, dx, ds) for dx, ds in planes[1:]]
    turned_gate, more_down = turned(
        place, pieces, [(gate_weight, True, everything), (down_weight, False, late)], depth
    )
    near_x = stacked([line_x] + from_x, 0, [turned_gate[0]])
    far_x = swap(near_x)
    from_g = [across(line_g, dx, ds) for dx, ds in planes[1:]]
    gate, up, weight, turned_up = gate_up(place, near_x, far_x, turned_gate, up_weight)
    near_g = stacked([line_g] + from_g, 0, [weight])
    far_g = swap(near_g)
    near_d, far_d, dgate, dup, hidw = middle(
        place, experts, pieces, near_g, far_g, weight, gate, up,
        turned_down + more_down, turned_gate, turned_up,
    )

    other_d = swap(far_d)
    chunks = depth // chunk_of(depth // pieces, GRAD_CHUNK)
    some = chunks // 5
    (gate_grad,) = weight_grads(place, pieces, near_x, far_x, depth, True, [(dgate, 0, some, None)])
    gate_grad, up_grad = weight_grads(
        place, pieces, near_x, far_x, depth, True,
        [(dgate, some, chunks, gate_grad), (dup, 0, chunks, None)],
    )
    (down_grad,) = weight_grads(
        place, pieces, near_g, far_g, depth, False, [(hidw, 0, chunks, None)]
    )

    blocks = pair_sums(near_d, other_d, experts, len(planes))
    arrived = [
        across(block, -dx, -ds) for block, (dx, ds) in zip(blocks[1:], planes[1:], strict=True)
    ]
    sends = plane_sums([blocks[0]] + arrived, experts, pieces)
    finals = [sends[0]] + [along(sends[k], -k) for k in range(1, pieces)]
    x_grad, routes = line_sums(finals, ids, experts)
    route_grad = routes.T
    return (x_grad, route_grad, gate_grad, up_grad, down_grad)


def solution(mesh):
    in_specs = (
        P(("expert", "seq"), "tensor"),
        P(("expert", "seq"), "tensor"),
        P(("expert", "seq"), None),
        P(("expert", "seq"), None),
        P("expert", None, ("seq", "tensor")),
        P("expert", None, ("seq", "tensor")),
        P("expert", ("seq", "tensor"), None),
    )
    out_specs = (
        P(("expert", "seq"), "tensor"),
        P(("expert", "seq"), None),
        P("expert", None, ("seq", "tensor")),
        P("expert", None, ("seq", "tensor")),
        P("expert", ("seq", "tensor"), None),
    )
    return jax.shard_map(
        per_device, mesh=mesh, in_specs=in_specs, out_specs=out_specs, check_vma=False
    )
```

```python
import functools

import jax
import jax.numpy as jnp
from jax import lax
from jax.experimental import pallas as pl
from jax.experimental.pallas import tpu as pltpu
from jax.sharding import PartitionSpec as P

EXTRA = 128
SLOTS = 6
TURN_CHUNK = 384
GRAD_CHUNK = 256
MIB = 1 << 20
PLAIN = (((1,), (0,)), ((), ()))
CONTRACT_ROWS = (((0,), (0,)), ((), ()))
CONTRACT_COLS = (((1,), (1,)), ((), ()))
VMEM = pl.BlockSpec(memory_space=pltpu.VMEM)
SMEM = pl.BlockSpec(memory_space=pltpu.SMEM)
ANY = pl.BlockSpec(memory_space=pl.ANY)
HBM = pl.BlockSpec(memory_space=pltpu.HBM)


def matmul(a, b, dims=PLAIN):
    return lax.dot_general(a, b, dims, preferred_element_type=jnp.float32)


def shaped(shape, dtype=jnp.bfloat16):
    return jax.ShapeDtypeStruct(shape, dtype)


def local_call(
    body, name, mib, flops, moved, in_specs, out_specs, out_shape, scratch=(), aliases=None
):
    return pl.pallas_call(
        body,
        in_specs=in_specs,
        out_specs=out_specs,
        out_shape=out_shape,
        scratch_shapes=list(scratch),
        input_output_aliases=aliases or {},
        compiler_params=pltpu.CompilerParams(vmem_limit_bytes=mib * MIB),
        cost_estimate=pl.CostEstimate(
            flops=int(flops), bytes_accessed=int(moved), transcendentals=0
        ),
        name=name,
    )


def chunk_of(features, most=768):
    for size in (768, 512, 384, 256, 128):
        if features % size == 0 and size <= most:
            return size
    return features


def whole_chunks(home, pieces, depth, most=768):
    width = depth // pieces
    size = chunk_of(width, most)
    found = []
    for k in range(pieces):
        owner = lax.rem(home - k + pieces, pieces)
        for c in range(width // size):
            start = pl.multiple_of(owner * width + c * size, size)
            found.append((k * width + c * size, start))
    return size, found


def both_rows(near, far, start, size):
    return jnp.concatenate([near[:, start : start + size], far[:, start : start + size]], axis=0)


def jobs_chunks(place, pieces, jobs, depth):
    width = depth // pieces
    size, chunks = whole_chunks(place[0], pieces, depth, TURN_CHUNK)
    found, base = [], 0
    for weight, by_rows, which in jobs:
        for rel, start in chunks:
            if rel // width in which:
                found.append((weight, by_rows, base + rel // width - which.start, rel % width, start))
        base += len(which)
    return size, found


def turn_into(out, base, value, by_rows):
    rows, columns = value.shape
    for at in range(0, columns, EXTRA):
        turned_part = value[:, at : at + EXTRA].T
        if by_rows:
            out[at : at + EXTRA, base : base + rows] = turned_part
        else:
            out[base + at : base + at + EXTRA, :] = turned_part


def turned_kernel(place, *refs, pieces, jobs, depth):
    weights = refs[: len(jobs)]
    count = sum(len(which) for _, _, which in jobs)
    *outs, flat, tall, sems = refs[-count - 3 :]
    jobs = [(w, by_rows, which) for w, (_, by_rows, which) in zip(weights, jobs, strict=True)]
    size, chunks = jobs_chunks(place, pieces, jobs, depth)

    def buffer(j):
        return (flat if chunks[j][1] else tall).at[j % SLOTS]

    def copy(j):
        weight, by_rows, _, _, start = chunks[j]
        span = pl.ds(start, size)
        source = weight.at[0, span] if by_rows else weight.at[0, :, span]
        return pltpu.make_async_copy(source, buffer(j), sems.at[j % SLOTS])

    for j in range(min(SLOTS, len(chunks))):
        copy(j).start()
    for j, (_, by_rows, out, base, _) in enumerate(chunks):
        copy(j).wait()
        turn_into(outs[out], base, buffer(j), by_rows)
        if j + SLOTS < len(chunks):
            copy(j + SLOTS).start()


def turned(place, pieces, jobs, depth, after=()):
    width = depth // pieces
    size = chunk_of(width, TURN_CHUNK)
    hidden = jobs[0][0].shape[2] if jobs[0][1] else jobs[0][0].shape[1]
    shapes = []
    for _, by_rows, which in jobs:
        shapes += [shaped((hidden, width) if by_rows else (width, hidden))] * len(which)
    kinds = {by_rows for _, by_rows, _ in jobs}
    weights = [pltpu.with_memory_space_constraint(w, pltpu.HBM) for w, _, _ in jobs]
    shared = functools.partial(
        turned_kernel, pieces=pieces, jobs=[(None, b, which) for _, b, which in jobs], depth=depth
    )
    found = local_call(
        shared,
        "turned",
        7 * len(kinds),
        0,
        0,
        [SMEM] + [HBM] * len(weights) + [ANY] * len(after),
        [VMEM] * len(shapes),
        shapes,
        [
            pltpu.VMEM((SLOTS if True in kinds else 1, size, hidden), jnp.bfloat16),
            pltpu.VMEM((SLOTS if False in kinds else 1, hidden, size), jnp.bfloat16),
            pltpu.SemaphoreType.DMA((SLOTS,)),
        ],
    )(place, *weights, *after)
    result, at = [], 0
    for _, _, which in jobs:
        result.append(found[at : at + len(which)])
        at += len(which)
    return result


def gate_up_kernel(place, xp, xo, wu, *refs, pieces):
    wg, refs = refs[:pieces], refs[pieces:]
    gate, up, weight, *outs, buf, sems = refs
    hidden, width = wg[0].shape
    size, chunks = whole_chunks(place[0], pieces, width * pieces)
    slots = buf.shape[0]

    def copy(j):
        span = pl.ds(chunks[j][1], size)
        return pltpu.make_async_copy(wu.at[0, span], buf.at[j % slots], sems.at[j % slots])

    for j in range(min(slots, len(chunks))):
        copy(j).start()
    for k, w in enumerate(wg):
        rows = both_rows(xp, xo, k * width, width)
        for at in range(0, hidden, EXTRA):
            value = matmul(rows, w[at : at + EXTRA, :], CONTRACT_COLS)
            if k == 0:
                gate[:, at : at + EXTRA] = value
            else:
                gate[:, at : at + EXTRA] += value
    lane = lax.broadcasted_iota(jnp.int32, (1, EXTRA), 1)
    mine = both_rows(xp, xo, width * pieces, EXTRA).astype(jnp.float32)
    total = jnp.sum(jnp.where(lane == place[1], mine, 0.0), axis=1, keepdims=True)
    weight[...] = jnp.broadcast_to(total, weight.shape)
    for j, (rel, _) in enumerate(chunks):
        copy(j).wait()
        piece = buf.at[j % slots]
        value = matmul(both_rows(xp, xo, rel, size), piece[...])
        if j == 0:
            up[...] = value
        else:
            up[...] += value
        turn_into(outs[rel // width], rel % width, piece, True)
        if j + slots < len(chunks):
            copy(j + slots).start()


def gate_up(place, near, far, turned_gate, w_up):
    half = near.shape[0]
    pieces = len(turned_gate)
    hidden, width = turned_gate[0].shape
    out = shaped((2 * half, hidden), jnp.float32)
    gate, up, weight, *turned_up = local_call(
        functools.partial(gate_up_kernel, pieces=pieces),
        "gate_up",
        10,
        0,
        0,
        [SMEM] + [VMEM] * 2 + [HBM] + [VMEM] * pieces,
        [VMEM] * (3 + pieces),
        [out, out, shaped((2 * half, EXTRA), jnp.float32)] + [shaped((hidden, width))] * pieces,
        [
            pltpu.VMEM((4, chunk_of(width), hidden), jnp.bfloat16),
            pltpu.SemaphoreType.DMA((4,)),
        ],
    )(place, near, far, pltpu.with_memory_space_constraint(w_up, pltpu.HBM), *turned_gate)
    return gate, up, weight, turned_up


def middle_kernel(
    place, gp, go, weight_in, gate, up, *refs, pieces, experts
):
    wd, wg, wu = refs[:pieces], refs[pieces : 2 * pieces], refs[2 * pieces : 3 * pieces]
    near, far, dgate, dup, hidw, raw = refs[3 * pieces :]
    width = wg[0].shape[1]
    half = near.shape[0]
    depth = width * pieces
    for k in range(pieces):
        value = matmul(both_rows(gp, go, k * width, width), wd[k][...])
        if k == 0:
            raw[...] = value
        else:
            raw[...] += value
    lane = lax.broadcasted_iota(jnp.int32, (1, EXTRA), 1)
    mine = lane == place[1]
    weight = weight_in[:, :1]
    gate_value = gate[...]
    up_value = up[...]
    raw_value = raw[...]
    sigmoid_gate = jax.nn.sigmoid(gate_value)
    activated = gate_value * sigmoid_gate
    hidden_value = activated * up_value
    scaled = weight * raw_value
    slope = sigmoid_gate * (1.0 + gate_value * (1.0 - sigmoid_gate))
    dgate[...] = (scaled * up_value * slope).astype(jnp.bfloat16)
    dup[...] = (scaled * activated).astype(jnp.bfloat16)
    hidw[...] = (weight * hidden_value).astype(jnp.bfloat16)
    total = jnp.sum(hidden_value * raw_value, axis=1, keepdims=True)
    high = total.astype(jnp.bfloat16).astype(jnp.float32)
    low = total - high
    placed = jnp.where(mine, high, 0.0) + jnp.where(lane == place[1] + experts, low, 0.0)
    placed = placed.astype(jnp.bfloat16)
    near[:, depth:] = placed[:half]
    far[:, depth:] = placed[half:]
    step = chunk_of(width)
    for at in range(0, depth, step):
        k, base = at // width, at % width
        span = slice(base, base + step)
        value = matmul(dgate[...], wg[k][:, span]) + matmul(dup[...], wu[k][:, span])
        value = value.astype(jnp.bfloat16)
        near[:, at : at + step] = value[:half]
        far[:, at : at + step] = value[half:]


def middle(place, experts, pieces, near, far, weight, gate, up, turned_down, turned_gate, turned_up):
    half = near.shape[0]
    hidden, width = turned_gate[0].shape
    depth = width * pieces
    out = shaped((2 * half, hidden))
    result = shaped((half, depth + EXTRA))
    return local_call(
        functools.partial(middle_kernel, pieces=pieces, experts=experts),
        "middle",
        4,
        0,
        0,
        [SMEM] + [VMEM] * (5 + 3 * pieces),
        [VMEM] * 5,
        [result, result, out, out, out],
        [pltpu.VMEM((2 * half, hidden), jnp.float32)],
    )(place, near, far, weight, gate, up, *turned_down, *turned_gate, *turned_up)


def weight_kernel(place, near, far, *refs, pieces, jobs, by_rows):
    deltas = refs[: len(jobs)]
    *outs, buf, sems = refs[-len(jobs) - 2 :]
    depth = outs[0].shape[1] if by_rows else outs[0].shape[2]
    size, chunks = whole_chunks(place[0], pieces, depth, GRAD_CHUNK)
    copies = []
    for delta, out, (first, last) in zip(deltas, outs, jobs, strict=True):
        for rel, start in chunks[first:last]:
            j = len(copies)
            rows = both_rows(near, far, rel, size)
            span = pl.ds(start, size)
            if by_rows:
                value, target = matmul(rows, delta[...], CONTRACT_ROWS), out.at[0, span]
            else:
                value, target = matmul(delta[...], rows, CONTRACT_ROWS), out.at[0, :, span]
            buf[j] = value.astype(jnp.bfloat16)
            copy = pltpu.make_async_copy(buf.at[j], target, sems.at[j])
            copy.start()
            copies.append(copy)
    for copy in copies:
        copy.wait()


def weight_grads(place, pieces, near, far, depth, by_rows, jobs):
    half = near.shape[0]
    hidden = jobs[0][0].shape[1]
    size = chunk_of(depth // pieces, GRAD_CHUNK)
    count = sum(last - first for _, first, last, _ in jobs)
    there = [(i, job[3]) for i, job in enumerate(jobs) if job[3] is not None]
    held = [pltpu.with_memory_space_constraint(g, pltpu.HBM) for _, g in there]
    return local_call(
        functools.partial(
            weight_kernel, pieces=pieces, jobs=[job[1:3] for job in jobs], by_rows=by_rows
        ),
        "weight_grads",
        4 + (count * size * hidden * 2) // MIB,
        4 * half * size * count * hidden,
        2 * size * count * hidden,
        [SMEM] + [VMEM] * (2 + len(jobs)) + [HBM] * len(held),
        [ANY] * len(jobs),
        [shaped((1, depth, hidden) if by_rows else (1, hidden, depth))] * len(jobs),
        [
            pltpu.VMEM((count, size, hidden) if by_rows else (count, hidden, size), jnp.bfloat16),
            pltpu.SemaphoreType.DMA((count,)),
        ],
        aliases={3 + len(jobs) + n: i for n, (i, _) in enumerate(there)},
    )(place, near, far, *[job[0] for job in jobs], *held)


def stack_kernel(*refs, axis, count):
    out = refs[-1]
    at = 0
    for ref in refs[:count]:
        size = ref.shape[axis]
        if axis:
            out[:, at : at + size] = ref[...]
        else:
            out[at : at + size, :] = ref[...]
        at += size


def stacked(blocks, axis, after=()):
    shape = list(blocks[0].shape)
    shape[axis] = sum(b.shape[axis] for b in blocks)
    count = shape[0] * shape[1]
    return local_call(
        functools.partial(stack_kernel, axis=axis, count=len(blocks)),
        "stacked",
        2,
        0,
        4 * count,
        [VMEM] * len(blocks) + [ANY] * len(after),
        VMEM,
        shaped(tuple(shape)),
    )(*blocks, *after)


def first_kernel(x, g, out, sems):
    rows = x.shape[0]
    copies = [
        pltpu.make_async_copy(ref, out.at[pl.ds(i * rows, rows)], sems.at[i])
        for i, ref in enumerate((x, g))
    ]
    for copy in copies:
        copy.start()
    for copy in copies:
        copy.wait()


def first_pair(x, g):
    rows, width = x.shape
    return local_call(
        first_kernel,
        "first_pair",
        1,
        0,
        8 * rows * width,
        [HBM] * 2,
        VMEM,
        shaped((2 * rows, width)),
        [pltpu.SemaphoreType.DMA((2,))],
    )(*(pltpu.with_memory_space_constraint(v, pltpu.HBM) for v in (x, g)))


def token_columns(table, ids, weights):
    choices, rows = ids.shape
    table[...] = jnp.zeros_like(table)
    table[:choices, :rows] = ids[...].astype(jnp.float32)
    if weights is not None:
        table[choices : 2 * choices, :rows] = weights[...].astype(jnp.float32)
    return table[...].T[:rows]


def line_pair_kernel(*refs):
    *blocks, ids, weights, _, line_x, line_g, table = refs
    rows = line_x.shape[0]
    width = blocks[0].shape[1]
    for k, block in enumerate(blocks):
        line_x[:, k * width : (k + 1) * width] = block[:rows, :]
        line_g[:, k * width : (k + 1) * width] = block[rows:, :]
    choices = ids.shape[0]
    columns = token_columns(table, ids, weights)
    lane = lax.broadcasted_iota(jnp.int32, (rows, EXTRA), 1).astype(jnp.float32)
    extra = jnp.zeros((rows, EXTRA), jnp.float32)
    for k in range(choices):
        hit = lane == columns[:, k : k + 1]
        extra += jnp.where(hit, columns[:, choices + k : choices + k + 1], 0.0)
    line_x[:, len(blocks) * width :] = extra.astype(jnp.bfloat16)


def line_pair(blocks, ids, weights, after):
    rows = ids.shape[1]
    depth = blocks[0].shape[1] * len(blocks)
    return local_call(
        line_pair_kernel,
        "line_pair",
        2,
        0,
        8 * rows * depth,
        [VMEM] * (len(blocks) + 2) + [ANY],
        [VMEM] * 2,
        [shaped((rows, depth + EXTRA)), shaped((rows, depth))],
        [pltpu.VMEM((8, EXTRA), jnp.float32)],
    )(*blocks, ids, weights, after)


def resplit(extra, experts):
    lane = lax.broadcasted_iota(jnp.int32, extra.shape, 1)
    total = extra + pltpu.roll(extra, EXTRA - experts, 1)
    total = jnp.where(lane < experts, total, 0.0)
    high = total.astype(jnp.bfloat16).astype(jnp.float32)
    return (high + pltpu.roll(total - high, experts, 1)).astype(jnp.bfloat16)


def pair_kernel(near, other, *outs, experts):
    rows, width = outs[0].shape
    depth = width - EXTRA
    for i, out in enumerate(outs):
        span = pl.ds(i * rows, rows)
        value = near[span, :].astype(jnp.float32) + other[span, :].astype(jnp.float32)
        out[:, :depth] = value[:, :depth].astype(jnp.bfloat16)
        out[:, depth:] = resplit(value[:, depth:], experts)


def pair_sums(near, other, experts, count):
    rows, width = near.shape[0] // count, near.shape[1]
    return local_call(
        functools.partial(pair_kernel, experts=experts),
        "pair_sums",
        2,
        0,
        6 * near.size,
        [VMEM] * 2,
        [VMEM] * count,
        [shaped((rows, width))] * count,
    )(near, other)


def plane_kernel(*refs, experts, pieces):
    blocks, outs = refs[:-pieces], refs[-pieces:]
    width = outs[0].shape[1] - EXTRA
    depth = width * pieces

    def total(start, size):
        values = [b[:, start : start + size].astype(jnp.float32) for b in blocks]
        return functools.reduce(lambda a, b: a + b, values)

    extra = resplit(total(depth, EXTRA), experts)
    for k, out in enumerate(outs):
        out[:, :width] = total(k * width, width).astype(jnp.bfloat16)
        out[:, width:] = extra


def plane_sums(blocks, experts, pieces):
    rows, width = blocks[0].shape[0], (blocks[0].shape[1] - EXTRA) // pieces + EXTRA
    return local_call(
        functools.partial(plane_kernel, experts=experts, pieces=pieces),
        "plane_sums",
        2,
        0,
        2 * blocks[0].size * len(blocks),
        [VMEM] * len(blocks),
        [VMEM] * pieces,
        [shaped((rows, width))] * pieces,
    )(*blocks)


def tree_sum(parts):
    while len(parts) > 1:
        middle = len(parts) // 2
        parts = [a + b for a, b in zip(parts[:middle], parts[middle:], strict=True)]
    return parts[0]


def line_kernel(*refs, experts):
    *blocks, ids, grads, routes, table = refs
    rows, width = grads.shape
    grads[...] = tree_sum([b[:, :width].astype(jnp.float32) for b in blocks]).astype(jnp.bfloat16)
    extra = tree_sum([b[:, width:].astype(jnp.float32) for b in blocks])
    total = extra + pltpu.roll(extra, EXTRA - experts, 1)
    total = total.astype(jnp.bfloat16).astype(jnp.float32)
    columns = token_columns(table, ids, None)
    lane = lax.broadcasted_iota(jnp.int32, (rows, EXTRA), 1)
    chosen = jnp.zeros((rows, EXTRA), jnp.float32)
    for k in range(ids.shape[0]):
        hit = lane.astype(jnp.float32) == columns[:, k : k + 1]
        value = jnp.sum(jnp.where(hit, total, 0.0), axis=1, keepdims=True)
        chosen += jnp.where(lane == k, value, 0.0)
    routes[...] = chosen.T[: ids.shape[0], :].astype(jnp.bfloat16)


def line_sums(blocks, ids, experts):
    rows, width = blocks[0].shape[0], blocks[0].shape[1] - EXTRA
    return local_call(
        functools.partial(line_kernel, experts=experts),
        "line_sums",
        2,
        0,
        2 * blocks[0].size * len(blocks),
        [VMEM] * (len(blocks) + 1),
        [VMEM] * 2,
        [shaped((rows, width)), shaped(ids.shape)],
        [pltpu.VMEM((8, EXTRA), jnp.float32)],
    )(*blocks, ids)


def per_device(tokens_in, out_grad, route_ids, route_weight, gate_weight, up_weight, down_weight):
    experts = lax.axis_size("expert")
    seqs = lax.axis_size("seq")
    pieces = lax.axis_size("tensor")
    depth = tokens_in.shape[1] * pieces
    place = jnp.stack([lax.axis_index("tensor"), lax.axis_index("expert")]).astype(jnp.int32)
    chips = experts // 2
    planes = [(dx, ds) for ds in range(seqs) for dx in range(chips)]

    def along(value, shift):
        pairs = [(i, (i + shift) % pieces) for i in range(pieces)]
        return lax.ppermute(value, "tensor", pairs)

    def across(value, dx, ds):
        pairs = []
        for e in range(experts):
            for s in range(seqs):
                to_e = ((e // 2 + dx) % chips) * 2 + e % 2
                pairs.append((e * seqs + s, to_e * seqs + (s + ds) % seqs))
        return lax.ppermute(value, ("expert", "seq"), pairs)

    def swap(value):
        return lax.ppermute(value, "expert", [(e, e ^ 1) for e in range(experts)])

    ids, choice_weights = route_ids.T, route_weight.T
    both = first_pair(tokens_in, out_grad)
    arrived = [along(both, k) for k in range(1, pieces)]
    everything = range(pieces)
    early, late = range(pieces // 2), range(pieces // 2, pieces)
    (turned_down,) = turned(place, pieces, [(down_weight, False, early)], depth)
    line_x, line_g = line_pair([both] + arrived, ids, choice_weights, turned_down[0])
    from_x = [across(line_x, dx, ds) for dx, ds in planes[1:]]
    turned_gate, more_down = turned(
        place, pieces, [(gate_weight, True, everything), (down_weight, False, late)], depth
    )
    near_x = stacked([line_x] + from_x, 0, [turned_gate[0]])
    far_x = swap(near_x)
    from_g = [across(line_g, dx, ds) for dx, ds in planes[1:]]
    gate, up, weight, turned_up = gate_up(place, near_x, far_x, turned_gate, up_weight)
    near_g = stacked([line_g] + from_g, 0, [weight])
    far_g = swap(near_g)
    near_d, far_d, dgate, dup, hidw = middle(
        place, experts, pieces, near_g, far_g, weight, gate, up,
        turned_down + more_down, turned_gate, turned_up,
    )

    other_d = swap(far_d)
    chunks = depth // chunk_of(depth // pieces, GRAD_CHUNK)
    some = chunks // 5
    (gate_grad,) = weight_grads(place, pieces, near_x, far_x, depth, True, [(dgate, 0, some, None)])
    gate_grad, up_grad = weight_grads(
        place, pieces, near_x, far_x, depth, True,
        [(dgate, some, chunks, gate_grad), (dup, 0, chunks, None)],
    )
    (down_grad,) = weight_grads(
        place, pieces, near_g, far_g, depth, False, [(hidw, 0, chunks, None)]
    )

    blocks = pair_sums(near_d, other_d, experts, len(planes))
    arrived = [
        across(block, -dx, -ds) for block, (dx, ds) in zip(blocks[1:], planes[1:], strict=True)
    ]
    sends = plane_sums([blocks[0]] + arrived, experts, pieces)
    finals = [sends[0]] + [along(sends[k], -k) for k in range(1, pieces)]
    x_grad, routes = line_sums(finals, ids, experts)
    route_grad = routes.T
    return (x_grad, route_grad, gate_grad, up_grad, down_grad)


def solution(mesh):
    in_specs = (
        P(("expert", "seq"), "tensor"),
        P(("expert", "seq"), "tensor"),
        P(("expert", "seq"), None),
        P(("expert", "seq"), None),
        P("expert", None, ("seq", "tensor")),
        P("expert", None, ("seq", "tensor")),
        P("expert", ("seq", "tensor"), None),
    )
    out_specs = (
        P(("expert", "seq"), "tensor"),
        P(("expert", "seq"), None),
        P("expert", None, ("seq", "tensor")),
        P("expert", None, ("seq", "tensor")),
        P("expert", ("seq", "tensor"), None),
    )
    return jax.shard_map(
        per_device, mesh=mesh, in_specs=in_specs, out_specs=out_specs, check_vma=False
    )
```
